32 devices in a mesh: row: 4 (over z), col: 8 (over y, x, core).
Axes of the slice: x: 2, y: 2, z: 4, core: 2. Of those that a mesh axis runs over, the one named last changes fastest.
Arguments:
- blocks: bfloat16 [4, 8, 192, 128, 128], P('row', 'col'), may hold values from -0.059814453 to 0.059814453
- block_rows: int32 [4, 8, 192], P('row', 'col'), may hold values from 0 to 255, as said below
- block_cols: int32 [4, 8, 192], P('row', 'col'), may hold values from 0 to 255, as said below
- counts: int32 [4, 8], P('row', 'col'), may hold values from 96 to 192, as said below
- travel_times: float32 [16, 131072], P(None, ('row', 'col')), may hold values from -6 to 6
Outputs:
- solution: float32 [16, 8, 4, 8192], P(None, 'col', 'row')
- scaled_direction: float32 [16, 8, 4, 8192], P(None, 'col', 'row')
The draws below stay inside these ranges and needn't reach their ends.
Inputs may be any that keep to these rules, and one draw needn't show every extreme that they name: Ray block of a slot within the 256 ray blocks of its row group; among the filled slots of one device the (block_rows, block_cols) pairs are all different. `block_cols`: cell block of a slot within the 256 cell blocks of its column group. `counts`: some device fills all 192 slots.
All inputs are finite; a program needn't handle non-finite values.
Results may differ from the reference program's by a relative error of at most 0.0054.
Values may be sent and summed in bfloat16 or wider, within the bound.
A program may use at most 64 MiB of HBM per device.

```python
import jax
import jax.numpy as jnp
from jax import lax

BS = 128
RB_DEV = 256
CB_DEV = 256
NB_DEV = 192
RHS = 16
ITERS = 2
ROWS = 131072
CELLS = 262144
CELL_DEV = 8192
N_ROW = 4
N_COL = 8


def pattern_pairs(key):
    subkeys = jax.random.split(jax.random.fold_in(key, 11), N_ROW * N_COL)
    chosen = jax.vmap(lambda subkey: jax.random.permutation(subkey, RB_DEV * CB_DEV))(subkeys)[:, :NB_DEV]
    return chosen.reshape(N_ROW, N_COL, NB_DEV).astype(jnp.int32)


def draw_block_rows(key, part):
    return pattern_pairs(key) // CB_DEV


def draw_block_cols(key, part):
    return pattern_pairs(key) % CB_DEV


def draw_counts(key, part):
    first_key, second_key = jax.random.split(jax.random.fold_in(key, 23))
    base = jax.random.randint(first_key, (N_ROW * N_COL,), NB_DEV // 2, NB_DEV + 1)
    fullest = jax.random.randint(second_key, (), 0, N_ROW * N_COL)
    places = jnp.arange(N_ROW * N_COL, dtype=jnp.int32)
    filled = jnp.where(places == fullest, NB_DEV, base)
    return filled.reshape(N_ROW, N_COL).astype(jnp.int32)


def levels(stream_key, extent, cuts, smallest, high):
    gain, own = 1.0, jax.random.fold_in(stream_key, 6)
    for axis_at, blocks in cuts:
        heights = jnp.exp(jax.random.uniform(jax.random.fold_in(own, axis_at), (blocks,), jnp.float32, smallest / len(cuts), high / len(cuts)))
        gain = gain * jnp.repeat(heights, extent[axis_at] // blocks).reshape([-1 if axis == axis_at else 1 for axis in range(len(extent))])
    return gain


def centred(key, shape, scale, limit, cuts=(), held_as=jnp.bfloat16):
    factor_of = levels(key, shape, cuts, -0.22, 0.18) if cuts else 1.0
    drawn = jax.random.normal(key, shape, jnp.float32) * scale * factor_of
    return jnp.minimum(jnp.maximum(drawn, -limit), limit).astype(held_as)


def setup_inputs(seed: int = 0) -> dict:
    key_list = jax.random.split(jax.random.key(seed), 6)
    return {
        "blocks": centred(key_list[0], (N_ROW, N_COL, NB_DEV, BS, BS), 0.01, 0.059814453, ((0, 4), (1, 8))),
        "block_rows": draw_block_rows(jax.random.fold_in(key_list[5], 71), 0),
        "block_cols": draw_block_cols(jax.random.fold_in(key_list[5], 71), 0),
        "counts": draw_counts(jax.random.fold_in(key_list[5], 71), 0),
        "travel_times": centred(key_list[4], (RHS, ROWS), 1.0, 6.0, ((1, 32),), jnp.float32),
    }


norm_eps = 1e-06

def rotation(rho_bar, phi_bar, beta_norm, alpha_norm):
    rho_new = jnp.sqrt(rho_bar * rho_bar + beta_norm * beta_norm)
    cosine = rho_bar / rho_new
    sine_val = beta_norm / rho_new
    theta_coef = sine_val * alpha_norm
    rho_next = -cosine * alpha_norm
    phi_new = cosine * phi_bar
    phi_next = sine_val * phi_bar
    return (phi_new / rho_new, theta_coef / rho_new, rho_next, phi_next)

def flat_inputs(blocks, block_rows, block_cols, counts):
    device_ids = jnp.arange(N_ROW * N_COL, dtype=jnp.int32)
    return (device_ids, blocks.reshape(N_ROW * N_COL, NB_DEV, BS, BS), block_rows.reshape(N_ROW * N_COL, NB_DEV), block_cols.reshape(N_ROW * N_COL, NB_DEV), counts.reshape(N_ROW * N_COL))

def hot_table(indices, count_here, width):
    filled = jnp.arange(NB_DEV, dtype=jnp.int32) < count_here
    return ((indices[None, :] == jnp.arange(width, dtype=jnp.int32)[:, None]) & filled[None, :]).astype(jnp.float32)

def apply_forward(items_all, right_full):
    count_rhs = right_full.shape[0]

    def visit(total, items):
        device_id, blocks_here, rows_here, cols_here, count_here = items
        row_group = device_id // N_COL
        col_group = device_id % N_COL
        segment = lax.dynamic_slice_in_dim(right_full, col_group * (CB_DEV * BS), CB_DEV * BS, 1)
        picked = jnp.take(segment.reshape(count_rhs, CB_DEV, BS), cols_here, axis=1)
        product = jnp.einsum('knj,nij->kni', picked.astype(jnp.float32), blocks_here.astype(jnp.float32), precision=lax.Precision.HIGHEST)
        row_hot = hot_table(rows_here, count_here, RB_DEV)
        part = jnp.einsum('rn,kni->kri', row_hot, product, precision=lax.Precision.HIGHEST).reshape(count_rhs, RB_DEV * BS)
        start = row_group * (RB_DEV * BS)
        current = lax.dynamic_slice_in_dim(total, start, RB_DEV * BS, 1)
        return (lax.dynamic_update_slice_in_dim(total, current + part, start, 1), None)
    return lax.scan(visit, jnp.zeros((count_rhs, ROWS), jnp.float32), items_all)[0]

def apply_backward(items_all, left_full):
    count_rhs = left_full.shape[0]

    def visit(total, items):
        device_id, blocks_here, rows_here, cols_here, count_here = items
        row_group = device_id // N_COL
        col_group = device_id % N_COL
        segment = lax.dynamic_slice_in_dim(left_full, row_group * (RB_DEV * BS), RB_DEV * BS, 1)
        picked = jnp.take(segment.reshape(count_rhs, RB_DEV, BS), rows_here, axis=1)
        product = jnp.einsum('kni,nij->knj', picked.astype(jnp.float32), blocks_here.astype(jnp.float32), precision=lax.Precision.HIGHEST)
        col_hot = hot_table(cols_here, count_here, CB_DEV)
        part = jnp.einsum('cn,knj->kcj', col_hot, product, precision=lax.Precision.HIGHEST).reshape(count_rhs, CB_DEV * BS)
        start = col_group * (CB_DEV * BS)
        current = lax.dynamic_slice_in_dim(total, start, CB_DEV * BS, 1)
        return (lax.dynamic_update_slice_in_dim(total, current + part, start, 1), None)
    return lax.scan(visit, jnp.zeros((count_rhs, CELLS), jnp.float32), items_all)[0]

def vector_norm(values):
    return jnp.sqrt(lax.optimization_barrier(jnp.sum(values * values, axis=1)) + norm_eps)

def reference(blocks, block_rows, block_cols, counts, travel_times):
    items_all = flat_inputs(blocks, block_rows, block_cols, counts)
    beta_norm = vector_norm(travel_times)
    left_vec = travel_times / beta_norm[:, None]
    cells_vec = apply_backward(items_all, left_vec.astype(jnp.bfloat16))
    alpha_norm = vector_norm(cells_vec)
    right_vec = cells_vec / alpha_norm[:, None]
    direction = right_vec
    solution = jnp.zeros_like(right_vec)
    phi_bar = beta_norm
    rho_bar = alpha_norm
    for iteration in range(ITERS):
        rays_vec = apply_forward(items_all, right_vec.astype(jnp.bfloat16)) - alpha_norm[:, None] * left_vec
        beta_norm = vector_norm(rays_vec)
        left_vec = rays_vec / beta_norm[:, None]
        cells_vec = apply_backward(items_all, left_vec.astype(jnp.bfloat16)) - beta_norm[:, None] * right_vec
        alpha_norm = vector_norm(cells_vec)
        right_vec = cells_vec / alpha_norm[:, None]
        step_scale, turn_scale, rho_bar, phi_bar = rotation(rho_bar, phi_bar, beta_norm, alpha_norm)
        solution = solution + step_scale[:, None] * direction
        direction = right_vec - turn_scale[:, None] * direction
    count_rhs = travel_times.shape[0]
    scaled = phi_bar[:, None] * direction
    return (solution.reshape(count_rhs, N_COL, N_ROW, CELL_DEV), scaled.reshape(count_rhs, N_COL, N_ROW, CELL_DEV))
```

```python
import functools

import jax
import jax.numpy as jnp
from jax import lax
from jax.experimental import pallas as pl
from jax.experimental.pallas import tpu as pltpu
from jax.sharding import PartitionSpec as P

BS = 128
RB_DEV = 256
CB_DEV = 256
ITERS = 2
UNROLL = 8

norm_eps = 1e-06


def rotation(rho_bar, phi_bar, beta_norm, alpha_norm):
    rho_new = jnp.sqrt(rho_bar * rho_bar + beta_norm * beta_norm)
    cosine = rho_bar / rho_new
    sine_val = beta_norm / rho_new
    theta_coef = sine_val * alpha_norm
    rho_next = -cosine * alpha_norm
    phi_new = cosine * phi_bar
    phi_next = sine_val * phi_bar
    return (phi_new / rho_new, theta_coef / rho_new, rho_next, phi_next)


def loop(count, body, init=None):
    step = UNROLL
    while count % step:
        step //= 2

    def several(chunk, carry):
        for k in range(step):
            carry = body(chunk * step + k, carry)
        return carry

    return lax.fori_loop(0, count // step, several, init)


def kernel(
    n_row, n_col, idx, keep, blocks_hbm, t_ref, sol_ref, dir_ref,
    blocks, prods, own, ray_a, ray_b, cells, gath, send, recv_row, recv_col,
    stat_send, stat_gather, stat_reduce, stat_row, stat_col,
    load_sem, ag_send, ag_recv, rs_send, rs_recv, sa_send, sa_recv, sr_send, sr_recv,
    fin_send, fin_recv,
):
    phases = 2 * ITERS + 1
    slots = blocks.shape[0]
    count_rhs = t_ref.shape[0]
    size = {"row": n_row, "col": n_col}
    me = {axis: lax.axis_index(axis) for axis in size}
    width = {"row": CB_DEV // n_row, "col": RB_DEV // n_col}

    def peer(axis, d):
        return {axis: lax.rem(me[axis] + d, size[axis])}

    load = pltpu.make_async_copy(blocks_hbm, blocks, load_sem)
    load.start()

    barrier = pltpu.get_barrier_semaphore()
    for axis in size:
        for d in range(1, size[axis]):
            pl.semaphore_signal(
                barrier, inc=1, device_id=peer(axis, d), device_id_type=pl.DeviceIdType.MESH
            )
    pl.semaphore_wait(barrier, n_row + n_col - 2)

    def push(src, dst, send_sem, recv_sem, axis, d):
        copy = pltpu.make_async_remote_copy(
            src_ref=src, dst_ref=dst, send_sem=send_sem, recv_sem=recv_sem,
            device_id=peer(axis, d), device_id_type=pl.DeviceIdType.MESH,
        )
        copy.start()
        return copy

    def gather(phase, axis, squares):
        w = width[axis]
        mine = pl.ds(pl.multiple_of(me[axis] * w, w), w)
        stat_send[phase] = squares
        copies = []
        for d in range(1, size[axis]):
            copies.append(push(
                gath.at[phase, mine], gath.at[phase, mine],
                ag_send.at[phase, d], ag_recv.at[phase, d], axis, d))
            copies.append(push(
                stat_send.at[phase], stat_gather.at[phase, d],
                sa_send.at[phase, d], sa_recv.at[phase, d], axis, d))
        for copy in copies:
            copy.wait()
        for d in range(1, size[axis]):
            squares = squares + stat_gather[phase, d]
        return squares

    def multiply(phase, direction):
        contract = (((1,), (0,)), ((), ())) if direction == 0 else (((1,), (1,)), ((), ()))

        def body(p, acc):
            x = gath[phase, idx[4 * direction + 1, p]]
            block = blocks[idx[4 * direction, p]]
            y = lax.dot_general(x, block, contract, preferred_element_type=jnp.float32)
            acc = acc * keep[direction, p] + y
            prods[p] = acc
            return acc

        loop(slots, body, jnp.zeros((count_rhs, BS), jnp.float32))

    def scatter(phase, direction, axis, squares, recv):
        w = width[axis]
        last = 4 * direction + 2
        copies = []
        stat_reduce[phase] = squares
        for d in range(1, size[axis]):
            first = lax.rem(me[axis] + d, size[axis]) * w

            def fill(j, carry):
                send[phase, first + j] = prods[idx[last, first + j]].astype(jnp.bfloat16)
                return carry

            loop(w, fill)
            copies.append(push(
                send.at[phase, pl.ds(pl.multiple_of(first, w), w)], recv.at[phase // 2, d],
                rs_send.at[phase, d], rs_recv.at[phase, d], axis, d))
            copies.append(push(
                stat_reduce.at[phase], (stat_row if axis == "row" else stat_col).at[phase // 2, d],
                sr_send.at[phase, d], sr_recv.at[phase, d], axis, d))
        mine = me[axis] * w

        def keep_own(j, carry):
            own[j] = prods[idx[last, mine + j]]
            return carry

        loop(w, keep_own)
        for copy in copies:
            copy.wait()
        for d in range(1, size[axis]):
            squares = squares + (stat_row if axis == "row" else stat_col)[phase // 2, d]
        return squares

    def norm(squares):
        total = jnp.sum(squares, axis=1, keepdims=True) + norm_eps
        return jnp.broadcast_to(jnp.sqrt(total), (count_rhs, BS))

    def everywhere(which, squares):
        for at, axis in enumerate(("row", "col")):
            slot = phases + 2 * which + at
            stat_send[slot] = squares
            copies = []
            for d in range(1, size[axis]):
                copies.append(push(
                    stat_send.at[slot], stat_gather.at[slot, d],
                    fin_send.at[2 * which + at, d], fin_recv.at[2 * which + at, d], axis, d))
            for copy in copies:
                copy.wait()
            for d in range(1, size[axis]):
                squares = squares + stat_gather[slot, d]
        return squares

    def update(phase, axis, recv, scale, store, previous, gather_phase):
        first = me[axis] * width[axis]

        def body(j, squares):
            total = own[j]
            for d in range(1, size[axis]):
                total = total + recv[phase // 2, d, j].astype(jnp.float32)
            value = total * scale - previous(j)
            store[j] = value
            if gather_phase is not None:
                gath[gather_phase, first + j] = value.astype(jnp.bfloat16)
            return squares + value * value

        return loop(width[axis], body, jnp.zeros((count_rhs, BS), jnp.float32))

    zeros = jnp.zeros((count_rhs, BS), jnp.float32)
    prods[slots] = zeros
    ray_now, ray_next = ray_a, ray_b
    first_ray = me["col"] * width["col"]

    squares = zeros
    for j in range(width["col"]):
        value = t_ref[:, j * BS : (j + 1) * BS]
        squares = squares + value * value
    beta = norm(everywhere(0, squares))
    for j in range(width["col"]):
        value = t_ref[:, j * BS : (j + 1) * BS] / beta
        ray_now[j] = value * beta
        gath[0, first_ray + j] = value.astype(jnp.bfloat16)

    squares = gather(0, "col", zeros)
    load.wait()
    multiply(0, 0)
    scatter(0, 0, "row", squares, recv_row)
    phi_bar = beta
    betas, alphas = [beta], []
    squares = update(0, "row", recv_row, 1.0, cells.at[0], lambda j: 0.0, 1)
    for iteration in range(ITERS):
        phase = 2 * iteration + 1
        squares = gather(phase, "row", squares)
        multiply(phase, 1)
        alpha = norm(scatter(phase, 1, "col", squares, recv_col))
        alphas.append(alpha)
        turn = alpha / beta
        squares = update(
            phase, "col", recv_col, 1.0 / alpha, ray_next, lambda j: ray_now[j] * turn, phase + 1)
        ray_now, ray_next = ray_next, ray_now
        phase = phase + 1
        squares = gather(phase, "col", squares)
        multiply(phase, 0)
        beta = norm(scatter(phase, 0, "row", squares, recv_row))
        betas.append(beta)
        turn = beta / alpha
        final = iteration == ITERS - 1
        squares = update(
            phase, "row", recv_row, 1.0 / beta, cells.at[iteration + 1],
            lambda j: cells[iteration, j] * turn, None if final else phase + 1)

    squares = everywhere(1, squares)
    alphas.append(norm(squares))

    rho_bar = alphas[0]
    rates, turns = [], []
    for iteration in range(ITERS):
        rate, turn, rho_bar, phi_bar = rotation(
            rho_bar, phi_bar, betas[iteration + 1], alphas[iteration + 1])
        rates.append(rate)
        turns.append(turn)

    def finish(j, carry):
        direction = cells[0, j] / alphas[0]
        total = zeros
        for iteration in range(ITERS):
            total = total + rates[iteration] * direction
            direction = cells[iteration + 1, j] / alphas[iteration + 1] - turns[iteration] * direction
        lanes = pl.ds(pl.multiple_of(j * BS, BS), BS)
        sol_ref[:, lanes] = total
        dir_ref[:, lanes] = phi_bar * direction
        return carry

    loop(width["row"], finish)


def order(key, other, filled):
    slots = key.shape[0]
    at = jnp.arange(slots, dtype=jnp.int32)
    key = jnp.where(filled, key, RB_DEV)
    other = jnp.where(filled, other, 0)
    before = (key[None, :] < key[:, None]) | ((key[None, :] == key[:, None]) & (at[None, :] < at[:, None]))
    rank = jnp.sum(before.astype(jnp.int32), axis=1)
    hot = (rank[None, :] == at[:, None]).astype(jnp.int32)
    perm = jnp.sum(hot * at[None, :], axis=1)
    other_sorted = jnp.sum(hot * other[None, :], axis=1)
    key_sorted = jnp.sum(hot * key[None, :], axis=1)
    same = jnp.concatenate([jnp.zeros((1,), bool), key_sorted[1:] == key_sorted[:-1]])
    outs = jnp.arange(RB_DEV, dtype=jnp.int32)[:, None]
    upto = jnp.sum((key[None, :] <= outs).astype(jnp.int32), axis=1)
    here = jnp.any(key[None, :] == outs, axis=1)
    last = jnp.where(here, upto - 1, slots)
    pad = RB_DEV - slots
    return (
        [jnp.pad(perm, (0, pad)), jnp.pad(other_sorted, (0, pad)), last, last],
        jnp.pad(same.astype(jnp.float32), (0, pad)),
    )


def shards(n_row, n_col, blocks, block_rows, block_cols, counts, travel_times):
    blocks_here = blocks[0, 0]
    rows_here = block_rows[0, 0]
    cols_here = block_cols[0, 0]
    slots = blocks_here.shape[0]
    count_rhs = travel_times.shape[0]
    filled = jnp.arange(slots, dtype=jnp.int32) < counts[0, 0]
    back, back_keep = order(cols_here, rows_here, filled)
    forth, forth_keep = order(rows_here, cols_here, filled)
    idx = jnp.stack(back + forth)
    keep = jnp.stack([back_keep, forth_keep])

    phases = 2 * ITERS + 1
    w_row, w_col = CB_DEV // n_row, RB_DEV // n_col
    n_max = max(n_row, n_col)
    tile = (count_rhs, BS)
    vmem, dma = pltpu.VMEM, pltpu.SemaphoreType.DMA
    f32, bf16 = jnp.float32, jnp.bfloat16
    out = jax.ShapeDtypeStruct((count_rhs, w_row * BS), f32)
    sol, direction = pl.pallas_call(
        functools.partial(kernel, n_row, n_col),
        out_shape=(out, out),
        in_specs=[
            pl.BlockSpec(memory_space=pltpu.SMEM),
            pl.BlockSpec(memory_space=pltpu.SMEM),
            pl.BlockSpec(memory_space=pl.ANY),
            pl.BlockSpec(memory_space=pltpu.VMEM),
        ],
        out_specs=(pl.BlockSpec(memory_space=pltpu.VMEM),) * 2,
        scratch_shapes=[
            vmem(blocks_here.shape, bf16),
            vmem((slots + 1, *tile), f32),
            vmem((max(w_row, w_col), *tile), f32),
            vmem((w_col, *tile), f32),
            vmem((w_col, *tile), f32),
            vmem((ITERS + 1, w_row, *tile), f32),
            vmem((phases, RB_DEV, *tile), bf16),
            vmem((phases, RB_DEV, *tile), bf16),
            vmem((ITERS + 1, n_row, w_row, *tile), bf16),
            vmem((ITERS, n_col, w_col, *tile), bf16),
            vmem((phases + 4, *tile), f32),
            vmem((phases + 4, n_max, *tile), f32),
            vmem((phases, *tile), f32),
            vmem((ITERS + 1, n_row, *tile), f32),
            vmem((ITERS, n_col, *tile), f32),
            dma,
            *[dma((phases, n_max))] * 8,
            *[dma((4, n_max))] * 2,
        ],
        compiler_params=pltpu.CompilerParams(
            collective_id=0, has_side_effects=True, vmem_limit_bytes=48 * 1024 * 1024
        ),
    )(idx, keep, blocks_here, travel_times)
    return (sol.reshape(count_rhs, 1, 1, -1), direction.reshape(count_rhs, 1, 1, -1))


def solution(mesh):
    placed = (
        P("row", "col", None, None, None),
        P("row", "col", None),
        P("row", "col", None),
        P("row", "col"),
        P(None, ("row", "col")),
    )
    return jax.shard_map(
        functools.partial(shards, mesh.shape["row"], mesh.shape["col"]),
        mesh=mesh,
        in_specs=placed,
        out_specs=(P(None, "col", "row", None), P(None, "col", "row", None)),
        check_vma=False,
    )
```

```python
import functools

import jax
import jax.numpy as jnp
from jax import lax
from jax.experimental import pallas as pl
from jax.experimental.pallas import tpu as pltpu
from jax.sharding import PartitionSpec as P

BS = 128
RB_DEV = 256
CB_DEV = 256
ITERS = 2
UNROLL = 8

norm_eps = 1e-06


def rotation(rho_bar, phi_bar, beta_norm, alpha_norm):
    rho_new = jnp.sqrt(rho_bar * rho_bar + beta_norm * beta_norm)
    cosine = rho_bar / rho_new
    sine_val = beta_norm / rho_new
    theta_coef = sine_val * alpha_norm
    rho_next = -cosine * alpha_norm
    phi_new = cosine * phi_bar
    phi_next = sine_val * phi_bar
    return (phi_new / rho_new, theta_coef / rho_new, rho_next, phi_next)


def loop(count, body, init=None):
    step = UNROLL
    while count % step:
        step //= 2

    def several(chunk, carry):
        for k in range(step):
            carry = body(chunk * step + k, carry)
        return carry

    return lax.fori_loop(0, count // step, several, init)


def kernel(
    n_row, n_col, idx, keep, blocks_hbm, t_ref, sol_ref, dir_ref,
    blocks, prods, own, ray_a, ray_b, cells, gath, send, transit, recv_row, core_send, core_recv, recv_col,
    stat_send, stat_gather, stat_reduce, stat_row, stat_col,
    load_sem, ag_send, ag_recv, ac_send, ac_recv, sa_send, sa_recv,
    tr_send, tr_recv, rs_send, rs_recv, sr_send, sr_recv, fin_send, fin_recv,
):
    phases = 2 * ITERS + 1
    slots = blocks.shape[0]
    count_rhs = t_ref.shape[0]
    size = {"row": n_row, "col": n_col}
    me = {axis: lax.axis_index(axis) for axis in size}
    width = {"row": CB_DEV // n_row, "col": RB_DEV // n_col}

    chips = n_col // 2

    def peer(axis, d):
        return {axis: lax.rem(me[axis] + d, size[axis])}

    load = pltpu.make_async_copy(blocks_hbm, blocks, load_sem)
    load.start()

    barrier = pltpu.get_barrier_semaphore()
    for axis in size:
        for d in range(1, size[axis]):
            pl.semaphore_signal(
                barrier, inc=1, device_id=peer(axis, d), device_id_type=pl.DeviceIdType.MESH
            )
    pl.semaphore_wait(barrier, n_row + n_col - 2)

    def push(src, dst, send_sem, recv_sem, axis, d):
        copy = pltpu.make_async_remote_copy(
            src_ref=src, dst_ref=dst, send_sem=send_sem, recv_sem=recv_sem,
            device_id=peer(axis, d), device_id_type=pl.DeviceIdType.MESH,
        )
        copy.start()
        return copy

    def share(axis, at):
        return pl.ds(pl.multiple_of(at * width[axis], width[axis]), width[axis])

    def send_squares(axis, squares, source, target, send_sem, recv_sem):
        source[...] = squares
        return [
            push(source, target.at[d], send_sem.at[d], recv_sem.at[d], axis, d)
            for d in range(1, size[axis])
        ]

    def add_squares(axis, squares, target, copies):
        for copy in copies:
            copy.wait()
        for d in range(1, size[axis]):
            squares = squares + target[d]
        return squares

    def gather_line(phase):
        me_row = me["row"]

        def hop(way, h):
            at = share("row", jnp.clip(me_row - way * h, 0, n_row - 1))
            lane = 0 if way > 0 else 1
            return pltpu.make_async_remote_copy(
                src_ref=gath.at[phase, at], dst_ref=gath.at[phase, at],
                send_sem=ag_send.at[phase, lane, h], recv_sem=ag_recv.at[phase, lane, h],
                device_id={"row": jnp.clip(me_row + way, 0, n_row - 1)},
                device_id_type=pl.DeviceIdType.MESH)

        def held(way, h):
            return (me_row >= h) if way > 0 else (me_row + h < n_row)

        def onward(way):
            return (me_row < n_row - 1) if way > 0 else (me_row > 0)

        for h in range(n_row):
            for way in (1, -1):
                if h:

                    @pl.when(held(way, h))
                    def _():
                        hop(way, h - 1).wait_recv()

                if h < n_row - 1:

                    @pl.when(held(way, h) & onward(way))
                    def _():
                        hop(way, h).start()

        for h in range(n_row - 1):
            for way in (1, -1):

                @pl.when(held(way, h) & onward(way))
                def _():
                    hop(way, h).wait_send()

    def gather_chips(phase):
        core = lax.rem(me["col"], 2)
        chip = me["col"] // 2
        copies, passed = [], []

        def across(e):
            at = share("col", me["col"])
            copy = pltpu.make_async_remote_copy(
                src_ref=gath.at[phase, at], dst_ref=gath.at[phase, at],
                send_sem=ag_send.at[phase, 0, e], recv_sem=ag_recv.at[phase, 0, e],
                device_id={"col": 2 * lax.rem(chip + e, chips) + core},
                device_id_type=pl.DeviceIdType.MESH)
            copy.start()
            return copy

        def pass_on(e):
            at = share("col", 2 * lax.rem(chip + chips - e, chips) + core)
            copy = pltpu.make_async_remote_copy(
                src_ref=gath.at[phase, at], dst_ref=gath.at[phase, at],
                send_sem=ac_send.at[phase, e], recv_sem=ac_recv.at[phase, e],
                device_id={"col": 2 * chip + 1 - core},
                device_id_type=pl.DeviceIdType.MESH)
            copy.start()
            return copy

        for e in range(1, chips):
            copies.append(across(e))
        passed.append(pass_on(0))
        for e in range(1, chips):
            copies[e - 1].wait_recv()
            passed.append(pass_on(e))
        for copy in passed:
            copy.wait()
        for copy in copies:
            copy.wait_send()

    def gather(phase, axis, squares):
        sums = send_squares(
            axis, squares, stat_send.at[phase], stat_gather.at[phase], sa_send.at[phase], sa_recv.at[phase])
        (gather_line if axis == "row" else gather_chips)(phase)
        return add_squares(axis, squares, stat_gather.at[phase], sums)

    def multiply(phase, direction):
        contract = (((1,), (0,)), ((), ())) if direction == 0 else (((1,), (1,)), ((), ()))

        def body(p, acc):
            x = gath[phase, idx[4 * direction + 1, p]]
            block = blocks[idx[4 * direction, p]]
            y = lax.dot_general(x, block, contract, preferred_element_type=jnp.float32)
            acc = acc * keep[direction, p] + y
            prods[p] = acc
            return acc

        loop(slots, body, jnp.zeros((count_rhs, BS), jnp.float32))

    def partial(direction, at):
        return prods[idx[4 * direction + 2, at]]

    def fill_send(phase, direction, first, count, arrived=None):
        def body(j, carry):
            value = partial(direction, first + j)
            if arrived is not None:
                value = value + arrived(j)
            send[phase, first + j] = value.astype(jnp.bfloat16)
            return carry

        loop(count, body)

    def scatter_line(phase):
        w = width["row"]
        me_row = me["row"]
        odd = lax.rem(me_row, 2)
        pair = me_row // 2
        partner = me_row + 1 - 2 * odd
        recv = recv_row.at[phase // 2]

        def leg(at, device, target, send_sem, recv_sem):
            return pltpu.make_async_remote_copy(
                src_ref=send.at[phase, share("row", at)], dst_ref=target,
                send_sem=send_sem, recv_sem=recv_sem,
                device_id={"row": device}, device_id_type=pl.DeviceIdType.MESH)

        def outer(i, upward):
            at = lax.select(upward, n_row - 1 - i, i)
            return at, lax.select(upward, at > 2 * pair + 1, at < 2 * pair)

        def first_leg(i):
            at, there = outer(i, odd == 0)
            return at, there, leg(
                at, partner, transit.at[phase // 2, i], tr_send.at[phase // 2, i], tr_recv.at[phase // 2, i])

        def second_leg(i):
            at, there = outer(i, odd == 1)
            return at, there, leg(
                at, at, recv.at[pair], rs_send.at[phase, 1 + i], rs_recv.at[phase, pair])

        for i in range(n_row - 2):
            at, there, copy = first_leg(i)

            @pl.when(there)
            def _():
                fill_send(phase, 0, at * w, w)
                copy.start()

        fill_send(phase, 0, partner * w, w)
        direct = leg(partner, partner, recv.at[pair], rs_send.at[phase, 0], rs_recv.at[phase, pair])
        direct.start()

        def keep_own(j, carry):
            own[j] = partial(0, me_row * w + j)
            return carry

        loop(w, keep_own)
        for i in range(n_row - 2):
            at, there, copy = second_leg(i)

            @pl.when(there)
            def _():
                pltpu.make_async_remote_copy(
                    src_ref=transit.at[phase // 2, i], dst_ref=transit.at[phase // 2, i],
                    send_sem=tr_send.at[phase // 2, i], recv_sem=tr_recv.at[phase // 2, i],
                    device_id={"row": partner}, device_id_type=pl.DeviceIdType.MESH).wait_recv()
                fill_send(phase, 0, at * w, w, lambda j: transit[phase // 2, i, j].astype(jnp.float32))
                copy.start()

        for m in range(n_row // 2):
            leg(partner, partner, recv.at[m], rs_send.at[phase, 0], rs_recv.at[phase, m]).wait_recv()
        direct.wait_send()
        for i in range(n_row - 2):
            for at, there, copy in (first_leg(i), second_leg(i)):

                @pl.when(there)
                def _():
                    copy.wait_send()

    def scatter_chips(phase):
        w = width["col"]
        core = lax.rem(me["col"], 2)
        chip = me["col"] // 2
        between, across = [], []
        for e in [*range(1, chips), 0]:
            first = (2 * lax.rem(chip + e, chips) + 1 - core) * w

            def body(j, carry):
                core_send[phase // 2, e, j] = partial(1, first + j)
                return carry

            loop(w, body)
            copy = pltpu.make_async_remote_copy(
                src_ref=core_send.at[phase // 2, e], dst_ref=core_recv.at[phase // 2, e],
                send_sem=tr_send.at[ITERS + 1 + phase // 2, e], recv_sem=tr_recv.at[ITERS + 1 + phase // 2, e],
                device_id={"col": 2 * chip + 1 - core}, device_id_type=pl.DeviceIdType.MESH)
            copy.start()
            between.append(copy)
        for e in range(1, chips):
            to = 2 * lax.rem(chip + e, chips) + core
            between[e - 1].wait_recv()
            fill_send(phase, 1, to * w, w, lambda j: core_recv[phase // 2, e, j])
            copy = pltpu.make_async_remote_copy(
                src_ref=send.at[phase, share("col", to)], dst_ref=recv_col.at[phase // 2, e],
                send_sem=rs_send.at[phase, e], recv_sem=rs_recv.at[phase, e],
                device_id={"col": to}, device_id_type=pl.DeviceIdType.MESH)
            copy.start()
            across.append(copy)
        between[-1].wait_recv()

        def keep_own(j, carry):
            own[j] = partial(1, me["col"] * w + j) + core_recv[phase // 2, 0, j]
            return carry

        loop(w, keep_own)
        for copy in across:
            copy.wait()
        for copy in between:
            copy.wait_send()

    def scatter(phase, axis, squares):
        target = stat_row if axis == "row" else stat_col
        sums = send_squares(
            axis, squares, stat_reduce.at[phase], target.at[phase // 2], sr_send.at[phase], sr_recv.at[phase])
        (scatter_line if axis == "row" else scatter_chips)(phase)
        return add_squares(axis, squares, target.at[phase // 2], sums)

    def norm(squares):
        total = jnp.sum(squares, axis=1, keepdims=True) + norm_eps
        return jnp.broadcast_to(jnp.sqrt(total), (count_rhs, BS))

    def everywhere(which, squares):
        for at, axis in enumerate(("row", "col")):
            slot, sem = phases + 2 * which + at, 2 * which + at
            sums = send_squares(
                axis, squares, stat_send.at[slot], stat_gather.at[slot], fin_send.at[sem], fin_recv.at[sem])
            squares = add_squares(axis, squares, stat_gather.at[slot], sums)
        return squares

    def update(phase, axis, recv, scale, store, previous, gather_phase):
        first = me[axis] * width[axis]

        def body(j, squares):
            total = own[j]
            for d in range(n_row // 2) if axis == "row" else range(1, chips):
                total = total + recv[phase // 2, d, j].astype(jnp.float32)
            value = total * scale - previous(j)
            store[j] = value
            if gather_phase is not None:
                gath[gather_phase, first + j] = value.astype(jnp.bfloat16)
            return squares + value * value

        return loop(width[axis], body, jnp.zeros((count_rhs, BS), jnp.float32))

    zeros = jnp.zeros((count_rhs, BS), jnp.float32)
    prods[slots] = zeros
    ray_now, ray_next = ray_a, ray_b
    first_ray = me["col"] * width["col"]

    squares = zeros
    for j in range(width["col"]):
        value = t_ref[:, j * BS : (j + 1) * BS]
        squares = squares + value * value
    beta = norm(everywhere(0, squares))
    for j in range(width["col"]):
        value = t_ref[:, j * BS : (j + 1) * BS]
        ray_now[j] = value
        gath[0, first_ray + j] = (value / beta).astype(jnp.bfloat16)

    squares = gather(0, "col", zeros)
    load.wait()
    multiply(0, 0)
    scatter(0, "row", squares)
    phi_bar = beta
    betas, alphas = [beta], []
    squares = update(0, "row", recv_row, 1.0, cells.at[0], lambda j: 0.0, 1)
    for iteration in range(ITERS):
        phase = 2 * iteration + 1
        squares = gather(phase, "row", squares)
        multiply(phase, 1)
        alpha = norm(scatter(phase, "col", squares))
        alphas.append(alpha)
        turn = alpha / beta
        squares = update(
            phase, "col", recv_col, 1.0 / alpha, ray_next, lambda j: ray_now[j] * turn, phase + 1)
        ray_now, ray_next = ray_next, ray_now
        phase = phase + 1
        squares = gather(phase, "col", squares)
        multiply(phase, 0)
        beta = norm(scatter(phase, "row", squares))
        betas.append(beta)
        turn = beta / alpha
        final = iteration == ITERS - 1
        squares = update(
            phase, "row", recv_row, 1.0 / beta, cells.at[iteration + 1],
            lambda j: cells[iteration, j] * turn, None if final else phase + 1)

    squares = everywhere(1, squares)
    alphas.append(norm(squares))

    rho_bar = alphas[0]
    rates, turns = [], []
    for iteration in range(ITERS):
        rate, turn, rho_bar, phi_bar = rotation(
            rho_bar, phi_bar, betas[iteration + 1], alphas[iteration + 1])
        rates.append(rate)
        turns.append(turn)

    def finish(j, carry):
        direction = cells[0, j] / alphas[0]
        total = zeros
        for iteration in range(ITERS):
            total = total + rates[iteration] * direction
            direction = cells[iteration + 1, j] / alphas[iteration + 1] - turns[iteration] * direction
        lanes = pl.ds(pl.multiple_of(j * BS, BS), BS)
        sol_ref[:, lanes] = total
        dir_ref[:, lanes] = phi_bar * direction
        return carry

    loop(width["row"], finish)


def order(key, other, filled):
    slots = key.shape[0]
    at = jnp.arange(slots, dtype=jnp.int32)
    key = jnp.where(filled, key, RB_DEV)
    other = jnp.where(filled, other, 0)
    before = (key[None, :] < key[:, None]) | ((key[None, :] == key[:, None]) & (at[None, :] < at[:, None]))
    rank = jnp.sum(before.astype(jnp.int32), axis=1)
    hot = (rank[None, :] == at[:, None]).astype(jnp.int32)
    perm = jnp.sum(hot * at[None, :], axis=1)
    other_sorted = jnp.sum(hot * other[None, :], axis=1)
    key_sorted = jnp.sum(hot * key[None, :], axis=1)
    same = jnp.concatenate([jnp.zeros((1,), bool), key_sorted[1:] == key_sorted[:-1]])
    outs = jnp.arange(RB_DEV, dtype=jnp.int32)[:, None]
    upto = jnp.sum((key[None, :] <= outs).astype(jnp.int32), axis=1)
    here = jnp.any(key[None, :] == outs, axis=1)
    last = jnp.where(here, upto - 1, slots)
    pad = RB_DEV - slots
    return (
        [jnp.pad(perm, (0, pad)), jnp.pad(other_sorted, (0, pad)), last, last],
        jnp.pad(same.astype(jnp.float32), (0, pad)),
    )


def shards(n_row, n_col, blocks, block_rows, block_cols, counts, travel_times):
    blocks_here = blocks[0, 0]
    rows_here = block_rows[0, 0]
    cols_here = block_cols[0, 0]
    slots = blocks_here.shape[0]
    count_rhs = travel_times.shape[0]
    filled = jnp.arange(slots, dtype=jnp.int32) < counts[0, 0]
    back, back_keep = order(cols_here, rows_here, filled)
    forth, forth_keep = order(rows_here, cols_here, filled)
    idx = jnp.stack(back + forth)
    keep = jnp.stack([back_keep, forth_keep])

    phases = 2 * ITERS + 1
    w_row, w_col = CB_DEV // n_row, RB_DEV // n_col
    n_max = max(n_row, n_col)
    tile = (count_rhs, BS)
    vmem, dma = pltpu.VMEM, pltpu.SemaphoreType.DMA
    f32, bf16 = jnp.float32, jnp.bfloat16
    out = jax.ShapeDtypeStruct((count_rhs, w_row * BS), f32)
    sol, direction = pl.pallas_call(
        functools.partial(kernel, n_row, n_col),
        out_shape=(out, out),
        in_specs=[
            pl.BlockSpec(memory_space=pltpu.SMEM),
            pl.BlockSpec(memory_space=pltpu.SMEM),
            pl.BlockSpec(memory_space=pl.ANY),
            pl.BlockSpec(memory_space=pltpu.VMEM),
        ],
        out_specs=(pl.BlockSpec(memory_space=pltpu.VMEM),) * 2,
        scratch_shapes=[
            vmem(blocks_here.shape, bf16),
            vmem((slots + 1, *tile), f32),
            vmem((max(w_row, w_col), *tile), f32),
            vmem((w_col, *tile), f32),
            vmem((w_col, *tile), f32),
            vmem((ITERS + 1, w_row, *tile), f32),
            vmem((phases, RB_DEV, *tile), bf16),
            vmem((phases, RB_DEV, *tile), bf16),
            vmem((ITERS + 1, n_row - 2, w_row, *tile), bf16),
            vmem((ITERS + 1, n_row // 2, w_row, *tile), bf16),
            vmem((ITERS, n_col // 2, w_col, *tile), f32),
            vmem((ITERS, n_col // 2, w_col, *tile), f32),
            vmem((ITERS, n_col // 2, w_col, *tile), bf16),
            vmem((phases + 4, *tile), f32),
            vmem((phases + 4, n_max, *tile), f32),
            vmem((phases, *tile), f32),
            vmem((ITERS + 1, n_row, *tile), f32),
            vmem((ITERS, n_col, *tile), f32),
            dma,
            *[dma((phases, 2, n_max))] * 2,
            *[dma((phases, n_max))] * 4,
            *[dma((2 * ITERS + 1, n_max))] * 2,
            *[dma((phases, n_max))] * 4,
            *[dma((4, n_max))] * 2,
        ],
        compiler_params=pltpu.CompilerParams(
            collective_id=0, has_side_effects=True, vmem_limit_bytes=48 * 1024 * 1024
        ),
    )(idx, keep, blocks_here, travel_times)
    return (sol.reshape(count_rhs, 1, 1, -1), direction.reshape(count_rhs, 1, 1, -1))


def solution(mesh):
    placed = (
        P("row", "col", None, None, None),
        P("row", "col", None),
        P("row", "col", None),
        P("row", "col"),
        P(None, ("row", "col")),
    )
    return jax.shard_map(
        functools.partial(shards, mesh.shape["row"], mesh.shape["col"]),
        mesh=mesh,
        in_specs=placed,
        out_specs=(P(None, "col", "row", None), P(None, "col", "row", None)),
        check_vma=False,
    )
```

```python
import functools

import jax
import jax.numpy as jnp
from jax import lax
from jax.experimental import pallas as pl
from jax.experimental.pallas import tpu as pltpu
from jax.sharding import PartitionSpec as P

BS = 128
RB_DEV = 256
CB_DEV = 256
ITERS = 2
UNROLL = 8

norm_eps = 1e-06


def rotation(rho_bar, phi_bar, beta_norm, alpha_norm):
    rho_new = jnp.sqrt(rho_bar * rho_bar + beta_norm * beta_norm)
    cosine = rho_bar / rho_new
    sine_val = beta_norm / rho_new
    theta_coef = sine_val * alpha_norm
    rho_next = -cosine * alpha_norm
    phi_new = cosine * phi_bar
    phi_next = sine_val * phi_bar
    return (phi_new / rho_new, theta_coef / rho_new, rho_next, phi_next)


def loop(count, read, write, init=None, step=UNROLL):
    while count % step:
        step //= 2

    def several(chunk, carry):
        values = [read(chunk * step + k) for k in range(step)]
        for k in range(step):
            carry = write(chunk * step + k, values[k], carry)
        return carry

    return lax.fori_loop(0, count // step, several, init)


def kernel(
    n_row, n_col, idx, keep, blocks_hbm, t_ref, sol_ref, dir_ref,
    blocks, prods, own, ray_a, ray_b, cells, gath, send, transit, recv_row, core_send, core_recv, recv_col,
    stat_send, stat_gather, stat_reduce, stat_row, stat_col,
    load_sem, ag_send, ag_recv, ac_send, ac_recv, sa_send, sa_recv,
    tr_send, tr_recv, rs_send, rs_recv, sr_send, sr_recv, fin_send, fin_recv,
):
    phases = 2 * ITERS + 1
    slots = blocks.shape[0]
    count_rhs = t_ref.shape[0]
    size = {"row": n_row, "col": n_col}
    me = {axis: lax.axis_index(axis) for axis in size}
    width = {"row": CB_DEV // n_row, "col": RB_DEV // n_col}

    chips = n_col // 2

    def peer(axis, d):
        return {axis: lax.rem(me[axis] + d, size[axis])}

    load = pltpu.make_async_copy(blocks_hbm, blocks, load_sem)
    load.start()

    barrier = pltpu.get_barrier_semaphore()
    for axis in size:
        for d in range(1, size[axis]):
            pl.semaphore_signal(
                barrier, inc=1, device_id=peer(axis, d), device_id_type=pl.DeviceIdType.MESH
            )
    pl.semaphore_wait(barrier, n_row + n_col - 2)

    def push(src, dst, send_sem, recv_sem, axis, d):
        copy = pltpu.make_async_remote_copy(
            src_ref=src, dst_ref=dst, send_sem=send_sem, recv_sem=recv_sem,
            device_id=peer(axis, d), device_id_type=pl.DeviceIdType.MESH,
        )
        copy.start()
        return copy

    def share(axis, at):
        return pl.ds(pl.multiple_of(at * width[axis], width[axis]), width[axis])

    def send_squares(axis, squares, source, target, send_sem, recv_sem):
        source[...] = squares
        return [
            push(source, target.at[d], send_sem.at[d], recv_sem.at[d], axis, d)
            for d in range(1, size[axis])
        ]

    def add_squares(axis, squares, target, copies):
        for copy in copies:
            copy.wait()
        for d in range(1, size[axis]):
            squares = squares + target[d]
        return squares

    def gather_line(phase):
        me_row = me["row"]

        def hop(way, h):
            at = share("row", jnp.clip(me_row - way * h, 0, n_row - 1))
            lane = 0 if way > 0 else 1
            return pltpu.make_async_remote_copy(
                src_ref=gath.at[phase, at], dst_ref=gath.at[phase, at],
                send_sem=ag_send.at[phase, lane, h], recv_sem=ag_recv.at[phase, lane, h],
                device_id={"row": jnp.clip(me_row + way, 0, n_row - 1)},
                device_id_type=pl.DeviceIdType.MESH)

        def held(way, h):
            return (me_row >= h) if way > 0 else (me_row + h < n_row)

        def onward(way):
            return (me_row < n_row - 1) if way > 0 else (me_row > 0)

        for h in range(n_row):
            for way in (1, -1):
                if h:

                    @pl.when(held(way, h))
                    def _():
                        hop(way, h - 1).wait_recv()

                if h < n_row - 1:

                    @pl.when(held(way, h) & onward(way))
                    def _():
                        hop(way, h).start()

        for h in range(n_row - 1):
            for way in (1, -1):

                @pl.when(held(way, h) & onward(way))
                def _():
                    hop(way, h).wait_send()

    def gather_chips(phase):
        core = lax.rem(me["col"], 2)
        chip = me["col"] // 2
        copies, passed = [], []

        def across(e):
            at = share("col", me["col"])
            copy = pltpu.make_async_remote_copy(
                src_ref=gath.at[phase, at], dst_ref=gath.at[phase, at],
                send_sem=ag_send.at[phase, 0, e], recv_sem=ag_recv.at[phase, 0, e],
                device_id={"col": 2 * lax.rem(chip + e, chips) + core},
                device_id_type=pl.DeviceIdType.MESH)
            copy.start()
            return copy

        def pass_on(e):
            at = share("col", 2 * lax.rem(chip + chips - e, chips) + core)
            copy = pltpu.make_async_remote_copy(
                src_ref=gath.at[phase, at], dst_ref=gath.at[phase, at],
                send_sem=ac_send.at[phase, e], recv_sem=ac_recv.at[phase, e],
                device_id={"col": 2 * chip + 1 - core},
                device_id_type=pl.DeviceIdType.MESH)
            copy.start()
            return copy

        for e in range(1, chips):
            copies.append(across(e))
        passed.append(pass_on(0))
        for e in range(1, chips):
            copies[e - 1].wait_recv()
            passed.append(pass_on(e))
        for copy in passed:
            copy.wait()
        for copy in copies:
            copy.wait_send()

    def gather(phase, axis, squares):
        sums = send_squares(
            axis, squares, stat_send.at[phase], stat_gather.at[phase], sa_send.at[phase], sa_recv.at[phase])
        (gather_line if axis == "row" else gather_chips)(phase)
        return add_squares(axis, squares, stat_gather.at[phase], sums)

    def multiply(phase, direction):
        contract = (((1,), (0,)), ((), ())) if direction == 0 else (((1,), (1,)), ((), ()))

        def read(p):
            x = gath[phase, idx[4 * direction + 1, p]]
            block = blocks[idx[4 * direction, p]]
            return lax.dot_general(x, block, contract, preferred_element_type=jnp.float32)

        def write(p, y, acc):
            acc = acc * keep[direction, p] + y
            prods[p] = acc
            return acc

        loop(slots, read, write, jnp.zeros((count_rhs, BS), jnp.float32), 16)

    def partial(direction, at):
        return prods[idx[4 * direction + 2, at]]

    def fill_send(phase, direction, first, count, arrived=None):
        def read(j):
            value = partial(direction, first + j)
            if arrived is not None:
                value = value + arrived(j)
            return value.astype(jnp.bfloat16)

        def write(j, value, carry):
            send[phase, first + j] = value

        loop(count, read, write)

    def scatter_line(phase):
        w = width["row"]
        me_row = me["row"]
        odd = lax.rem(me_row, 2)
        pair = me_row // 2
        partner = me_row + 1 - 2 * odd
        recv = recv_row.at[phase // 2]

        def leg(at, device, target, send_sem, recv_sem):
            return pltpu.make_async_remote_copy(
                src_ref=send.at[phase, share("row", at)], dst_ref=target,
                send_sem=send_sem, recv_sem=recv_sem,
                device_id={"row": device}, device_id_type=pl.DeviceIdType.MESH)

        def outer(i, upward):
            at = lax.select(upward, n_row - 1 - i, i)
            return at, lax.select(upward, at > 2 * pair + 1, at < 2 * pair)

        def first_leg(i):
            at, there = outer(i, odd == 0)
            return at, there, leg(
                at, partner, transit.at[phase // 2, i], tr_send.at[phase // 2, i], tr_recv.at[phase // 2, i])

        def second_leg(i):
            at, there = outer(i, odd == 1)
            return at, there, leg(
                at, at, recv.at[pair], rs_send.at[phase, 1 + i], rs_recv.at[phase, pair])

        for i in range(n_row - 2):
            at, there, copy = first_leg(i)

            @pl.when(there)
            def _():
                fill_send(phase, 0, at * w, w)
                copy.start()

        fill_send(phase, 0, partner * w, w)
        direct = leg(partner, partner, recv.at[pair], rs_send.at[phase, 0], rs_recv.at[phase, pair])
        direct.start()

        def keep_own(j, value, carry):
            own[j] = value

        loop(w, lambda j: partial(0, me_row * w + j), keep_own)
        for i in range(n_row - 2):
            at, there, copy = second_leg(i)

            @pl.when(there)
            def _():
                pltpu.make_async_remote_copy(
                    src_ref=transit.at[phase // 2, i], dst_ref=transit.at[phase // 2, i],
                    send_sem=tr_send.at[phase // 2, i], recv_sem=tr_recv.at[phase // 2, i],
                    device_id={"row": partner}, device_id_type=pl.DeviceIdType.MESH).wait_recv()
                fill_send(phase, 0, at * w, w, lambda j: transit[phase // 2, i, j].astype(jnp.float32))
                copy.start()

        for m in range(n_row // 2):
            leg(partner, partner, recv.at[m], rs_send.at[phase, 0], rs_recv.at[phase, m]).wait_recv()
        direct.wait_send()
        for i in range(n_row - 2):
            for at, there, copy in (first_leg(i), second_leg(i)):

                @pl.when(there)
                def _():
                    copy.wait_send()

    def scatter_chips(phase):
        w = width["col"]
        core = lax.rem(me["col"], 2)
        chip = me["col"] // 2
        between, across = [], []
        for e in [*range(1, chips), 0]:
            first = (2 * lax.rem(chip + e, chips) + 1 - core) * w

            def stage(j, value, carry):
                core_send[phase // 2, e, j] = value

            loop(w, lambda j: partial(1, first + j), stage)
            copy = pltpu.make_async_remote_copy(
                src_ref=core_send.at[phase // 2, e], dst_ref=core_recv.at[phase // 2, e],
                send_sem=tr_send.at[ITERS + 1 + phase // 2, e], recv_sem=tr_recv.at[ITERS + 1 + phase // 2, e],
                device_id={"col": 2 * chip + 1 - core}, device_id_type=pl.DeviceIdType.MESH)
            copy.start()
            between.append(copy)
        for e in range(1, chips):
            to = 2 * lax.rem(chip + e, chips) + core
            between[e - 1].wait_recv()
            fill_send(phase, 1, to * w, w, lambda j: core_recv[phase // 2, e, j])
            copy = pltpu.make_async_remote_copy(
                src_ref=send.at[phase, share("col", to)], dst_ref=recv_col.at[phase // 2, e],
                send_sem=rs_send.at[phase, e], recv_sem=rs_recv.at[phase, e],
                device_id={"col": to}, device_id_type=pl.DeviceIdType.MESH)
            copy.start()
            across.append(copy)
        between[-1].wait_recv()

        def keep_own(j, value, carry):
            own[j] = value

        loop(w, lambda j: partial(1, me["col"] * w + j) + core_recv[phase // 2, 0, j], keep_own)
        for copy in across:
            copy.wait()
        for copy in between:
            copy.wait_send()

    def scatter(phase, axis, squares):
        target = stat_row if axis == "row" else stat_col
        sums = send_squares(
            axis, squares, stat_reduce.at[phase], target.at[phase // 2], sr_send.at[phase], sr_recv.at[phase])
        (scatter_line if axis == "row" else scatter_chips)(phase)
        return add_squares(axis, squares, target.at[phase // 2], sums)

    def norm(squares):
        total = jnp.sum(squares, axis=1, keepdims=True) + norm_eps
        return jnp.broadcast_to(jnp.sqrt(total), (count_rhs, BS))

    def everywhere(which, squares):
        for at, axis in enumerate(("row", "col")):
            slot, sem = phases + 2 * which + at, 2 * which + at
            sums = send_squares(
                axis, squares, stat_send.at[slot], stat_gather.at[slot], fin_send.at[sem], fin_recv.at[sem])
            squares = add_squares(axis, squares, stat_gather.at[slot], sums)
        return squares

    def update(phase, axis, recv, scale, store, previous, gather_phase):
        first = me[axis] * width[axis]

        def read(j):
            total = own[j]
            for d in range(n_row // 2) if axis == "row" else range(1, chips):
                total = total + recv[phase // 2, d, j].astype(jnp.float32)
            return total * scale - previous(j)

        def write(j, value, squares):
            store[j] = value
            if gather_phase is not None:
                gath[gather_phase, first + j] = value.astype(jnp.bfloat16)
            return squares + value * value

        return loop(width[axis], read, write, jnp.zeros((count_rhs, BS), jnp.float32))

    zeros = jnp.zeros((count_rhs, BS), jnp.float32)
    prods[slots] = zeros
    ray_now, ray_next = ray_a, ray_b
    first_ray = me["col"] * width["col"]

    squares = zeros
    for j in range(width["col"]):
        value = t_ref[:, j * BS : (j + 1) * BS]
        squares = squares + value * value
    beta = norm(everywhere(0, squares))
    for j in range(width["col"]):
        value = t_ref[:, j * BS : (j + 1) * BS]
        ray_now[j] = value
        gath[0, first_ray + j] = (value / beta).astype(jnp.bfloat16)

    squares = gather(0, "col", zeros)
    load.wait()
    multiply(0, 0)
    scatter(0, "row", squares)
    phi_bar = beta
    betas, alphas = [beta], []
    squares = update(0, "row", recv_row, 1.0, cells.at[0], lambda j: 0.0, 1)
    for iteration in range(ITERS):
        phase = 2 * iteration + 1
        squares = gather(phase, "row", squares)
        multiply(phase, 1)
        alpha = norm(scatter(phase, "col", squares))
        alphas.append(alpha)
        turn = alpha / beta
        squares = update(
            phase, "col", recv_col, 1.0 / alpha, ray_next, lambda j: ray_now[j] * turn, phase + 1)
        ray_now, ray_next = ray_next, ray_now
        phase = phase + 1
        squares = gather(phase, "col", squares)
        multiply(phase, 0)
        beta = norm(scatter(phase, "row", squares))
        betas.append(beta)
        turn = beta / alpha
        final = iteration == ITERS - 1
        squares = update(
            phase, "row", recv_row, 1.0 / beta, cells.at[iteration + 1],
            lambda j: cells[iteration, j] * turn, None if final else phase + 1)

    squares = everywhere(1, squares)
    alphas.append(norm(squares))

    rho_bar = alphas[0]
    rates, turns = [], []
    for iteration in range(ITERS):
        rate, turn, rho_bar, phi_bar = rotation(
            rho_bar, phi_bar, betas[iteration + 1], alphas[iteration + 1])
        rates.append(rate)
        turns.append(turn)

    def finish(j):
        direction = cells[0, j] / alphas[0]
        total = zeros
        for iteration in range(ITERS):
            total = total + rates[iteration] * direction
            direction = cells[iteration + 1, j] / alphas[iteration + 1] - turns[iteration] * direction
        return total, phi_bar * direction

    def emit(j, values, carry):
        lanes = pl.ds(pl.multiple_of(j * BS, BS), BS)
        sol_ref[:, lanes], dir_ref[:, lanes] = values

    loop(width["row"], finish, emit, step=4)


def order(key, other, filled):
    slots = key.shape[0]
    at = jnp.arange(slots, dtype=jnp.int32)
    key = jnp.where(filled, key, RB_DEV)
    other = jnp.where(filled, other, 0)
    before = (key[None, :] < key[:, None]) | ((key[None, :] == key[:, None]) & (at[None, :] < at[:, None]))
    rank = jnp.sum(before.astype(jnp.int32), axis=1)
    hot = (rank[None, :] == at[:, None]).astype(jnp.int32)
    perm = jnp.sum(hot * at[None, :], axis=1)
    other_sorted = jnp.sum(hot * other[None, :], axis=1)
    key_sorted = jnp.sum(hot * key[None, :], axis=1)
    same = jnp.concatenate([jnp.zeros((1,), bool), key_sorted[1:] == key_sorted[:-1]])
    outs = jnp.arange(RB_DEV, dtype=jnp.int32)[:, None]
    upto = jnp.sum((key[None, :] <= outs).astype(jnp.int32), axis=1)
    here = jnp.any(key[None, :] == outs, axis=1)
    last = jnp.where(here, upto - 1, slots)
    pad = RB_DEV - slots
    return (
        [jnp.pad(perm, (0, pad)), jnp.pad(other_sorted, (0, pad)), last, last],
        jnp.pad(same.astype(jnp.float32), (0, pad)),
    )


def shards(n_row, n_col, blocks, block_rows, block_cols, counts, travel_times):
    blocks_here = blocks[0, 0]
    rows_here = block_rows[0, 0]
    cols_here = block_cols[0, 0]
    slots = blocks_here.shape[0]
    count_rhs = travel_times.shape[0]
    filled = jnp.arange(slots, dtype=jnp.int32) < counts[0, 0]
    back, back_keep = order(cols_here, rows_here, filled)
    forth, forth_keep = order(rows_here, cols_here, filled)
    idx = jnp.stack(back + forth)
    keep = jnp.stack([back_keep, forth_keep])

    phases = 2 * ITERS + 1
    w_row, w_col = CB_DEV // n_row, RB_DEV // n_col
    n_max = max(n_row, n_col)
    tile = (count_rhs, BS)
    vmem, dma = pltpu.VMEM, pltpu.SemaphoreType.DMA
    f32, bf16 = jnp.float32, jnp.bfloat16
    out = jax.ShapeDtypeStruct((count_rhs, w_row * BS), f32)
    sol, direction = pl.pallas_call(
        functools.partial(kernel, n_row, n_col),
        out_shape=(out, out),
        in_specs=[
            pl.BlockSpec(memory_space=pltpu.SMEM),
            pl.BlockSpec(memory_space=pltpu.SMEM),
            pl.BlockSpec(memory_space=pl.ANY),
            pl.BlockSpec(memory_space=pltpu.VMEM),
        ],
        out_specs=(pl.BlockSpec(memory_space=pltpu.VMEM),) * 2,
        scratch_shapes=[
            vmem(blocks_here.shape, bf16),
            vmem((slots + 1, *tile), f32),
            vmem((max(w_row, w_col), *tile), f32),
            vmem((w_col, *tile), f32),
            vmem((w_col, *tile), f32),
            vmem((ITERS + 1, w_row, *tile), f32),
            vmem((phases, RB_DEV, *tile), bf16),
            vmem((phases, RB_DEV, *tile), bf16),
            vmem((ITERS + 1, n_row - 2, w_row, *tile), bf16),
            vmem((ITERS + 1, n_row // 2, w_row, *tile), bf16),
            vmem((ITERS, n_col // 2, w_col, *tile), f32),
            vmem((ITERS, n_col // 2, w_col, *tile), f32),
            vmem((ITERS, n_col // 2, w_col, *tile), bf16),
            vmem((phases + 4, *tile), f32),
            vmem((phases + 4, n_max, *tile), f32),
            vmem((phases, *tile), f32),
            vmem((ITERS + 1, n_row, *tile), f32),
            vmem((ITERS, n_col, *tile), f32),
            dma,
            *[dma((phases, 2, n_max))] * 2,
            *[dma((phases, n_max))] * 4,
            *[dma((2 * ITERS + 1, n_max))] * 2,
            *[dma((phases, n_max))] * 4,
            *[dma((4, n_max))] * 2,
        ],
        compiler_params=pltpu.CompilerParams(
            collective_id=0, has_side_effects=True, vmem_limit_bytes=48 * 1024 * 1024
        ),
    )(idx, keep, blocks_here, travel_times)
    return (sol.reshape(count_rhs, 1, 1, -1), direction.reshape(count_rhs, 1, 1, -1))


def solution(mesh):
    placed = (
        P("row", "col", None, None, None),
        P("row", "col", None),
        P("row", "col", None),
        P("row", "col"),
        P(None, ("row", "col")),
    )
    return jax.shard_map(
        functools.partial(shards, mesh.shape["row"], mesh.shape["col"]),
        mesh=mesh,
        in_specs=placed,
        out_specs=(P(None, "col", "row", None), P(None, "col", "row", None)),
        check_vma=False,
    )
```

```python
import functools

import jax
import jax.numpy as jnp
from jax import lax
from jax.experimental import pallas as pl
from jax.experimental.pallas import tpu as pltpu
from jax.sharding import PartitionSpec as P

BS = 128
RB_DEV = 256
CB_DEV = 256
ITERS = 2
UNROLL = 8
HALVES = 2
LEAD = 0

norm_eps = 1e-06


def rotation(rho_bar, phi_bar, beta_norm, alpha_norm):
    rho_new = jnp.sqrt(rho_bar * rho_bar + beta_norm * beta_norm)
    cosine = rho_bar / rho_new
    sine_val = beta_norm / rho_new
    theta_coef = sine_val * alpha_norm
    rho_next = -cosine * alpha_norm
    phi_new = cosine * phi_bar
    phi_next = sine_val * phi_bar
    return (phi_new / rho_new, theta_coef / rho_new, rho_next, phi_next)


def loop(count, read, write, init=None, step=UNROLL):
    while count % step:
        step //= 2

    def several(chunk, carry):
        values = [read(chunk * step + k) for k in range(step)]
        for k in range(step):
            carry = write(chunk * step + k, values[k], carry)
        return carry

    return lax.fori_loop(0, count // step, several, init)


def kernel(
    n_row, n_col, idx, keep, blocks_hbm, t_ref, sol_ref, dir_ref, blocks, load_sem, *scratch
):
    gaths, scratch = scratch[:HALVES], scratch[HALVES:]
    size = {"row": n_row, "col": n_col}
    load = pltpu.make_async_copy(blocks_hbm, blocks, load_sem)
    load.start()

    barrier = pltpu.get_barrier_semaphore()
    for axis in size:
        for d in range(1, size[axis]):
            pl.semaphore_signal(
                barrier, inc=1, device_id={axis: lax.rem(lax.axis_index(axis) + d, size[axis])},
                device_id_type=pl.DeviceIdType.MESH,
            )
    pl.semaphore_wait(barrier, n_row + n_col - 2)

    programs = [
        half(g, n_row, n_col, load if g == 0 else None, idx, keep, t_ref, sol_ref, dir_ref, blocks,
             gaths[g], *[ref.at[g] for ref in scratch])
        for g in range(HALVES)
    ]
    for _ in range(LEAD):
        next(programs[0])
    while programs:
        programs = [program for program in programs if next(program, True) is None]


def half(
    g, n_row, n_col, load, idx, keep, t_ref, sol_ref, dir_ref, blocks,
    gath, prods, own, ray_a, ray_b, cells, send, transit, recv_row, core_send, core_recv, recv_col,
    stat_send, stat_gather, stat_reduce, stat_row, stat_col,
    ag_send, ag_recv, ac_send, ac_recv, sa_send, sa_recv,
    tr_send, tr_recv, rs_send, rs_recv, sr_send, sr_recv, fin_send, fin_recv,
):
    phases = 2 * ITERS + 1
    slots = blocks.shape[0]
    count_rhs = t_ref.shape[0] // HALVES
    tile = (2 * count_rhs, BS)
    mine = slice(g * count_rhs, (g + 1) * count_rhs)
    size = {"row": n_row, "col": n_col}
    me = {axis: lax.axis_index(axis) for axis in size}
    width = {"row": CB_DEV // n_row // 2, "col": RB_DEV // n_col // 2}

    chips = n_col // 2

    def peer(axis, d):
        return {axis: lax.rem(me[axis] + d, size[axis])}

    def push(src, dst, send_sem, recv_sem, axis, d):
        copy = pltpu.make_async_remote_copy(
            src_ref=src, dst_ref=dst, send_sem=send_sem, recv_sem=recv_sem,
            device_id=peer(axis, d), device_id_type=pl.DeviceIdType.MESH,
        )
        copy.start()
        return copy

    def share(axis, at):
        return pl.ds(pl.multiple_of(at * width[axis], width[axis]), width[axis])

    def send_squares(axis, squares, source, target, send_sem, recv_sem):
        source[...] = squares
        return [
            push(source, target.at[d], send_sem.at[d], recv_sem.at[d], axis, d)
            for d in range(1, size[axis])
        ]

    def add_squares(axis, squares, target, copies):
        for copy in copies:
            copy.wait()
        for d in range(1, size[axis]):
            squares = squares + target[d]
        return squares

    def gather_line(phase):
        me_row = me["row"]

        def hop(way, h):
            at = share("row", jnp.clip(me_row - way * h, 0, n_row - 1))
            lane = 0 if way > 0 else 1
            return pltpu.make_async_remote_copy(
                src_ref=gath.at[phase, at], dst_ref=gath.at[phase, at],
                send_sem=ag_send.at[phase, lane, h], recv_sem=ag_recv.at[phase, lane, h],
                device_id={"row": jnp.clip(me_row + way, 0, n_row - 1)},
                device_id_type=pl.DeviceIdType.MESH)

        def held(way, h):
            return (me_row >= h) if way > 0 else (me_row + h < n_row)

        def onward(way):
            return (me_row < n_row - 1) if way > 0 else (me_row > 0)

        for h in range(n_row):
            if h:
                yield
            for way in (1, -1):
                if h:

                    @pl.when(held(way, h))
                    def _():
                        hop(way, h - 1).wait_recv()

                if h < n_row - 1:

                    @pl.when(held(way, h) & onward(way))
                    def _():
                        hop(way, h).start()

        for h in range(n_row - 1):
            for way in (1, -1):

                @pl.when(held(way, h) & onward(way))
                def _():
                    hop(way, h).wait_send()

    def gather_chips(phase):
        core = lax.rem(me["col"], 2)
        chip = me["col"] // 2
        copies, passed = [], []

        def across(e):
            at = share("col", me["col"])
            copy = pltpu.make_async_remote_copy(
                src_ref=gath.at[phase, at], dst_ref=gath.at[phase, at],
                send_sem=ag_send.at[phase, 0, e], recv_sem=ag_recv.at[phase, 0, e],
                device_id={"col": 2 * lax.rem(chip + e, chips) + core},
                device_id_type=pl.DeviceIdType.MESH)
            copy.start()
            return copy

        def pass_on(e):
            at = share("col", 2 * lax.rem(chip + chips - e, chips) + core)
            copy = pltpu.make_async_remote_copy(
                src_ref=gath.at[phase, at], dst_ref=gath.at[phase, at],
                send_sem=ac_send.at[phase, e], recv_sem=ac_recv.at[phase, e],
                device_id={"col": 2 * chip + 1 - core},
                device_id_type=pl.DeviceIdType.MESH)
            copy.start()
            return copy

        for e in range(1, chips):
            copies.append(across(e))
        passed.append(pass_on(0))
        yield
        for e in range(1, chips):
            copies[e - 1].wait_recv()
            passed.append(pass_on(e))
        yield
        for copy in passed:
            copy.wait()
        for copy in copies:
            copy.wait_send()

    def gather(phase, axis, squares):
        sums = send_squares(
            axis, squares, stat_send.at[phase], stat_gather.at[phase], sa_send.at[phase], sa_recv.at[phase])
        yield from (gather_line if axis == "row" else gather_chips)(phase)
        return add_squares(axis, squares, stat_gather.at[phase], sums)

    def multiply(phase, direction):
        contract = (((1,), (0,)), ((), ())) if direction == 0 else (((1,), (1,)), ((), ()))

        def read(p):
            x = gath[phase, idx[4 * direction + 1, p]]
            block = blocks[idx[4 * direction, p]]
            y = lax.dot_general(x, block, contract, preferred_element_type=jnp.float32)
            second = keep[2 + direction, p]
            return y[:count_rhs] * (1.0 - second) + y[count_rhs:] * second

        def write(p, y, acc):
            acc = acc * keep[direction, p] + y
            prods[p] = acc
            return acc

        loop(slots, read, write, jnp.zeros((count_rhs, BS), jnp.float32), 16)

    def partial(direction, at):
        first = idx[4 * direction + 2, 2 * at]
        second = idx[4 * direction + 2, 2 * at + 1]
        return jnp.concatenate([prods[first], prods[second]], axis=0)

    def fill_send(phase, direction, first, count, arrived=None):
        def read(j):
            value = partial(direction, first + j)
            if arrived is not None:
                value = value + arrived(j)
            return value.astype(jnp.bfloat16)

        def write(j, value, carry):
            send[phase, first + j] = value

        loop(count, read, write)

    def scatter_line(phase):
        w = width["row"]
        me_row = me["row"]
        odd = lax.rem(me_row, 2)
        pair = me_row // 2
        partner = me_row + 1 - 2 * odd
        recv = recv_row.at[phase // 2]

        def leg(at, device, target, send_sem, recv_sem):
            return pltpu.make_async_remote_copy(
                src_ref=send.at[phase, share("row", at)], dst_ref=target,
                send_sem=send_sem, recv_sem=recv_sem,
                device_id={"row": device}, device_id_type=pl.DeviceIdType.MESH)

        def outer(i, upward):
            at = lax.select(upward, n_row - 1 - i, i)
            return at, lax.select(upward, at > 2 * pair + 1, at < 2 * pair)

        def first_leg(i):
            at, there = outer(i, odd == 0)
            return at, there, leg(
                at, partner, transit.at[phase // 2, i], tr_send.at[phase // 2, i], tr_recv.at[phase // 2, i])

        def second_leg(i):
            at, there = outer(i, odd == 1)
            return at, there, leg(
                at, at, recv.at[pair], rs_send.at[phase, 1 + i], rs_recv.at[phase, pair])

        for i in range(n_row - 2):
            at, there, copy = first_leg(i)

            @pl.when(there)
            def _():
                fill_send(phase, 0, at * w, w)
                copy.start()

        fill_send(phase, 0, partner * w, w)
        direct = leg(partner, partner, recv.at[pair], rs_send.at[phase, 0], rs_recv.at[phase, pair])
        direct.start()

        def keep_own(j, value, carry):
            own[j] = value

        loop(w, lambda j: partial(0, me_row * w + j), keep_own)
        for i in range(n_row - 2):
            yield
            at, there, copy = second_leg(i)

            @pl.when(there)
            def _():
                pltpu.make_async_remote_copy(
                    src_ref=transit.at[phase // 2, i], dst_ref=transit.at[phase // 2, i],
                    send_sem=tr_send.at[phase // 2, i], recv_sem=tr_recv.at[phase // 2, i],
                    device_id={"row": partner}, device_id_type=pl.DeviceIdType.MESH).wait_recv()
                fill_send(phase, 0, at * w, w, lambda j: transit[phase // 2, i, j].astype(jnp.float32))
                copy.start()

        yield
        for m in range(n_row // 2):
            leg(partner, partner, recv.at[m], rs_send.at[phase, 0], rs_recv.at[phase, m]).wait_recv()
        direct.wait_send()
        for i in range(n_row - 2):
            for at, there, copy in (first_leg(i), second_leg(i)):

                @pl.when(there)
                def _():
                    copy.wait_send()

    def scatter_chips(phase):
        w = width["col"]
        core = lax.rem(me["col"], 2)
        chip = me["col"] // 2
        between, across = [], []
        for e in [*range(1, chips), 0]:
            first = (2 * lax.rem(chip + e, chips) + 1 - core) * w

            def stage(j, value, carry):
                core_send[phase // 2, e, j] = value

            loop(w, lambda j: partial(1, first + j), stage)
            copy = pltpu.make_async_remote_copy(
                src_ref=core_send.at[phase // 2, e], dst_ref=core_recv.at[phase // 2, e],
                send_sem=tr_send.at[ITERS + 1 + phase // 2, e], recv_sem=tr_recv.at[ITERS + 1 + phase // 2, e],
                device_id={"col": 2 * chip + 1 - core}, device_id_type=pl.DeviceIdType.MESH)
            copy.start()
            between.append(copy)
        yield
        for e in range(1, chips):
            to = 2 * lax.rem(chip + e, chips) + core
            between[e - 1].wait_recv()
            fill_send(phase, 1, to * w, w, lambda j: core_recv[phase // 2, e, j])
            copy = pltpu.make_async_remote_copy(
                src_ref=send.at[phase, share("col", to)], dst_ref=recv_col.at[phase // 2, e],
                send_sem=rs_send.at[phase, e], recv_sem=rs_recv.at[phase, e],
                device_id={"col": to}, device_id_type=pl.DeviceIdType.MESH)
            copy.start()
            across.append(copy)
        between[-1].wait_recv()

        def keep_own(j, value, carry):
            own[j] = value

        loop(w, lambda j: partial(1, me["col"] * w + j) + core_recv[phase // 2, 0, j], keep_own)
        yield
        for copy in across:
            copy.wait()
        for copy in between:
            copy.wait_send()

    def scatter(phase, axis, squares):
        target = stat_row if axis == "row" else stat_col
        sums = send_squares(
            axis, squares, stat_reduce.at[phase], target.at[phase // 2], sr_send.at[phase], sr_recv.at[phase])
        yield from (scatter_line if axis == "row" else scatter_chips)(phase)
        return add_squares(axis, squares, target.at[phase // 2], sums)

    def norm(squares):
        total = jnp.sum(squares[:count_rhs] + squares[count_rhs:], axis=1, keepdims=True) + norm_eps
        value = jnp.broadcast_to(jnp.sqrt(total), (count_rhs, BS))
        return jnp.concatenate([value, value], axis=0)

    def everywhere(which, squares):
        for at, axis in enumerate(("row", "col")):
            slot, sem = phases + 2 * which + at, 2 * which + at
            sums = send_squares(
                axis, squares, stat_send.at[slot], stat_gather.at[slot], fin_send.at[sem], fin_recv.at[sem])
            yield
            squares = add_squares(axis, squares, stat_gather.at[slot], sums)
        return squares

    def update(phase, axis, recv, scale, store, previous, gather_phase):
        first = me[axis] * width[axis]

        def read(j):
            total = own[j]
            for d in range(n_row // 2) if axis == "row" else range(1, chips):
                total = total + recv[phase // 2, d, j].astype(jnp.float32)
            return total * scale - previous(j)

        def write(j, value, squares):
            store[j] = value
            if gather_phase is not None:
                gath[gather_phase, first + j] = value.astype(jnp.bfloat16)
            return squares + value * value

        return loop(width[axis], read, write, jnp.zeros(tile, jnp.float32))

    zeros = jnp.zeros(tile, jnp.float32)
    prods[slots] = zeros[:count_rhs]
    ray_now, ray_next = ray_a, ray_b
    first_ray = me["col"] * width["col"]

    def travel_times(j):
        lanes = [slice((2 * j + k) * BS, (2 * j + k + 1) * BS) for k in range(2)]
        return jnp.concatenate([t_ref[mine, lanes[0]], t_ref[mine, lanes[1]]], axis=0)

    squares = zeros
    for j in range(width["col"]):
        value = travel_times(j)
        squares = squares + value * value
    squares = yield from everywhere(0, squares)
    beta = norm(squares)
    for j in range(width["col"]):
        value = travel_times(j)
        ray_now[j] = value
        gath[0, first_ray + j] = (value / beta).astype(jnp.bfloat16)

    squares = yield from gather(0, "col", zeros)
    if load is not None:
        load.wait()
    multiply(0, 0)
    yield from scatter(0, "row", squares)
    phi_bar = beta
    betas, alphas = [beta], []
    squares = update(0, "row", recv_row, 1.0, cells.at[0], lambda j: 0.0, 1)
    for iteration in range(ITERS):
        phase = 2 * iteration + 1
        squares = yield from gather(phase, "row", squares)
        multiply(phase, 1)
        alpha = norm((yield from scatter(phase, "col", squares)))
        alphas.append(alpha)
        turn = alpha / beta
        squares = update(
            phase, "col", recv_col, 1.0 / alpha, ray_next, lambda j: ray_now[j] * turn, phase + 1)
        ray_now, ray_next = ray_next, ray_now
        phase = phase + 1
        squares = yield from gather(phase, "col", squares)
        multiply(phase, 0)
        beta = norm((yield from scatter(phase, "row", squares)))
        betas.append(beta)
        turn = beta / alpha
        final = iteration == ITERS - 1
        squares = update(
            phase, "row", recv_row, 1.0 / beta, cells.at[iteration + 1],
            lambda j: cells[iteration, j] * turn, None if final else phase + 1)

    squares = yield from everywhere(1, squares)
    alphas.append(norm(squares))

    rho_bar = alphas[0]
    rates, turns = [], []
    for iteration in range(ITERS):
        rate, turn, rho_bar, phi_bar = rotation(
            rho_bar, phi_bar, betas[iteration + 1], alphas[iteration + 1])
        rates.append(rate)
        turns.append(turn)

    def finish(j):
        direction = cells[0, j] / alphas[0]
        total = zeros
        for iteration in range(ITERS):
            total = total + rates[iteration] * direction
            direction = cells[iteration + 1, j] / alphas[iteration + 1] - turns[iteration] * direction
        return total, phi_bar * direction

    def emit(j, values, carry):
        for k in range(2):
            lanes = pl.ds(pl.multiple_of((2 * j + k) * BS, BS), BS)
            rows = slice(k * count_rhs, (k + 1) * count_rhs)
            sol_ref[mine, lanes], dir_ref[mine, lanes] = values[0][rows], values[1][rows]

    loop(width["row"], finish, emit, step=4)


def order(key, other, filled):
    slots = key.shape[0]
    at = jnp.arange(slots, dtype=jnp.int32)
    key = jnp.where(filled, key, RB_DEV)
    other = jnp.where(filled, other, 0)
    before = (key[None, :] < key[:, None]) | ((key[None, :] == key[:, None]) & (at[None, :] < at[:, None]))
    rank = jnp.sum(before.astype(jnp.int32), axis=1)
    hot = (rank[None, :] == at[:, None]).astype(jnp.int32)
    perm = jnp.sum(hot * at[None, :], axis=1)
    other_sorted = jnp.sum(hot * other[None, :], axis=1)
    key_sorted = jnp.sum(hot * key[None, :], axis=1)
    same = jnp.concatenate([jnp.zeros((1,), bool), key_sorted[1:] == key_sorted[:-1]])
    outs = jnp.arange(RB_DEV, dtype=jnp.int32)[:, None]
    upto = jnp.sum((key[None, :] <= outs).astype(jnp.int32), axis=1)
    here = jnp.any(key[None, :] == outs, axis=1)
    last = jnp.where(here, upto - 1, slots)
    pad = RB_DEV - slots
    return (
        [jnp.pad(perm, (0, pad)), jnp.pad(other_sorted // 2, (0, pad)), last, last],
        jnp.pad(same.astype(jnp.float32), (0, pad)),
        jnp.pad((other_sorted % 2).astype(jnp.float32), (0, pad)),
    )


def shards(n_row, n_col, blocks, block_rows, block_cols, counts, travel_times):
    blocks_here = blocks[0, 0]
    rows_here = block_rows[0, 0]
    cols_here = block_cols[0, 0]
    slots = blocks_here.shape[0]
    count_rhs = travel_times.shape[0]
    filled = jnp.arange(slots, dtype=jnp.int32) < counts[0, 0]
    back, back_keep, back_second = order(cols_here, rows_here, filled)
    forth, forth_keep, forth_second = order(rows_here, cols_here, filled)
    idx = jnp.stack(back + forth)
    keep = jnp.stack([back_keep, forth_keep, back_second, forth_second])

    phases = 2 * ITERS + 1
    w_row, w_col = CB_DEV // n_row // 2, RB_DEV // n_col // 2
    n_max = max(n_row, n_col)
    tile = (2 * count_rhs // HALVES, BS)
    vmem, dma = pltpu.VMEM, pltpu.SemaphoreType.DMA
    f32, bf16 = jnp.float32, jnp.bfloat16
    out = jax.ShapeDtypeStruct((count_rhs, 2 * w_row * BS), f32)
    sol, direction = pl.pallas_call(
        functools.partial(kernel, n_row, n_col),
        out_shape=(out, out),
        in_specs=[
            pl.BlockSpec(memory_space=pltpu.SMEM),
            pl.BlockSpec(memory_space=pltpu.SMEM),
            pl.BlockSpec(memory_space=pl.ANY),
            pl.BlockSpec(memory_space=pltpu.VMEM),
        ],
        out_specs=(pl.BlockSpec(memory_space=pltpu.VMEM),) * 2,
        scratch_shapes=[
            vmem(blocks_here.shape, bf16),
            dma,
            *[vmem((phases, RB_DEV // 2, *tile), bf16)] * HALVES,
            vmem((HALVES, slots + 1, count_rhs // HALVES, BS), f32),
            vmem((HALVES, max(w_row, w_col), *tile), f32),
            vmem((HALVES, w_col, *tile), f32),
            vmem((HALVES, w_col, *tile), f32),
            vmem((HALVES, ITERS + 1, w_row, *tile), f32),
            vmem((HALVES, phases, RB_DEV // 2, *tile), bf16),
            vmem((HALVES, ITERS + 1, n_row - 2, w_row, *tile), bf16),
            vmem((HALVES, ITERS + 1, n_row // 2, w_row, *tile), bf16),
            vmem((HALVES, ITERS, n_col // 2, w_col, *tile), f32),
            vmem((HALVES, ITERS, n_col // 2, w_col, *tile), f32),
            vmem((HALVES, ITERS, n_col // 2, w_col, *tile), bf16),
            vmem((HALVES, phases + 4, *tile), f32),
            vmem((HALVES, phases + 4, n_max, *tile), f32),
            vmem((HALVES, phases, *tile), f32),
            vmem((HALVES, ITERS + 1, n_row, *tile), f32),
            vmem((HALVES, ITERS, n_col, *tile), f32),
            *[dma((HALVES, phases, 2, n_max))] * 2,
            *[dma((HALVES, phases, n_max))] * 4,
            *[dma((HALVES, 2 * ITERS + 1, n_max))] * 2,
            *[dma((HALVES, phases, n_max))] * 4,
            *[dma((HALVES, 4, n_max))] * 2,
        ],
        compiler_params=pltpu.CompilerParams(
            collective_id=0, has_side_effects=True, vmem_limit_bytes=48 * 1024 * 1024
        ),
    )(idx, keep, blocks_here, travel_times)
    return (sol.reshape(count_rhs, 1, 1, -1), direction.reshape(count_rhs, 1, 1, -1))


def solution(mesh):
    placed = (
        P("row", "col", None, None, None),
        P("row", "col", None),
        P("row", "col", None),
        P("row", "col"),
        P(None, ("row", "col")),
    )
    return jax.shard_map(
        functools.partial(shards, mesh.shape["row"], mesh.shape["col"]),
        mesh=mesh,
        in_specs=placed,
        out_specs=(P(None, "col", "row", None), P(None, "col", "row", None)),
        check_vma=False,
    )
```

```python
import functools

import jax
import jax.numpy as jnp
from jax import lax
from jax.experimental import pallas as pl
from jax.experimental.pallas import tpu as pltpu
from jax.sharding import PartitionSpec as P

BS = 128
RB_DEV = 256
CB_DEV = 256
ITERS = 2
UNROLL = 8
HALVES = 2
LEAD = 0

norm_eps = 1e-06


def rotation(rho_bar, phi_bar, beta_norm, alpha_norm):
    rho_new = jnp.sqrt(rho_bar * rho_bar + beta_norm * beta_norm)
    cosine = rho_bar / rho_new
    sine_val = beta_norm / rho_new
    theta_coef = sine_val * alpha_norm
    rho_next = -cosine * alpha_norm
    phi_new = cosine * phi_bar
    phi_next = sine_val * phi_bar
    return (phi_new / rho_new, theta_coef / rho_new, rho_next, phi_next)


def loop(count, read, write, init=None, step=UNROLL):
    while count % step:
        step //= 2

    def several(chunk, carry):
        values = [read(chunk * step + k) for k in range(step)]
        for k in range(step):
            carry = write(chunk * step + k, values[k], carry)
        return carry

    return lax.fori_loop(0, count // step, several, init)


def kernel(
    n_row, n_col, idx, keep, blocks_hbm, t_ref, sol_ref, dir_ref, blocks, load_sem, *scratch
):
    gaths, scratch = scratch[:HALVES], scratch[HALVES:]
    size = {"row": n_row, "col": n_col}
    load = pltpu.make_async_copy(blocks_hbm, blocks, load_sem)
    load.start()

    barrier = pltpu.get_barrier_semaphore()
    for axis in size:
        for d in range(1, size[axis]):
            pl.semaphore_signal(
                barrier, inc=1, device_id={axis: lax.rem(lax.axis_index(axis) + d, size[axis])},
                device_id_type=pl.DeviceIdType.MESH,
            )
    pl.semaphore_wait(barrier, n_row + n_col - 2)

    programs = [
        half(g, n_row, n_col, load if g == 0 else None, idx, keep, t_ref, sol_ref, dir_ref, blocks,
             gaths[g], *[ref.at[g] for ref in scratch])
        for g in range(HALVES)
    ]
    for _ in range(LEAD):
        next(programs[0])
    while programs:
        programs = [program for program in programs if next(program, True) is None]


def half(
    g, n_row, n_col, load, idx, keep, t_ref, sol_ref, dir_ref, blocks,
    gath, prods, own, ray_a, ray_b, cells, send, transit, recv_row, core_send, core_recv, recv_col,
    stat_send, stat_gather, stat_reduce, stat_row, stat_col,
    ag_send, ag_recv, ac_send, ac_recv, sa_send, sa_recv,
    tr_send, tr_recv, rs_send, rs_recv, sr_send, sr_recv, fin_send, fin_recv,
):
    phases = 2 * ITERS + 1
    slots = blocks.shape[0]
    count_rhs = t_ref.shape[0] // HALVES
    tile = (2 * count_rhs, BS)
    mine = slice(g * count_rhs, (g + 1) * count_rhs)
    size = {"row": n_row, "col": n_col}
    me = {axis: lax.axis_index(axis) for axis in size}
    width = {"row": CB_DEV // n_row // 2, "col": RB_DEV // n_col // 2}

    chips = n_col // 2

    def peer(axis, d):
        return {axis: lax.rem(me[axis] + d, size[axis])}

    def push(src, dst, send_sem, recv_sem, axis, d):
        copy = pltpu.make_async_remote_copy(
            src_ref=src, dst_ref=dst, send_sem=send_sem, recv_sem=recv_sem,
            device_id=peer(axis, d), device_id_type=pl.DeviceIdType.MESH,
        )
        copy.start()
        return copy

    def share(axis, at):
        return pl.ds(pl.multiple_of(at * width[axis], width[axis]), width[axis])

    def send_squares(axis, squares, source, target, send_sem, recv_sem):
        source[...] = squares
        return [
            push(source, target.at[d], send_sem.at[d], recv_sem.at[d], axis, d)
            for d in range(1, size[axis])
        ]

    def add_squares(axis, squares, target, copies):
        for copy in copies:
            copy.wait()
        for d in range(1, size[axis]):
            squares = squares + target[d]
        return squares

    def gather_line(phase):
        me_row = me["row"]

        def hop(way, h):
            at = share("row", jnp.clip(me_row - way * h, 0, n_row - 1))
            lane = 0 if way > 0 else 1
            return pltpu.make_async_remote_copy(
                src_ref=gath.at[phase, at], dst_ref=gath.at[phase, at],
                send_sem=ag_send.at[phase, lane, h], recv_sem=ag_recv.at[phase, lane, h],
                device_id={"row": jnp.clip(me_row + way, 0, n_row - 1)},
                device_id_type=pl.DeviceIdType.MESH)

        def held(way, h):
            return (me_row >= h) if way > 0 else (me_row + h < n_row)

        def onward(way):
            return (me_row < n_row - 1) if way > 0 else (me_row > 0)

        for h in range(n_row):
            if h:
                yield
            for way in (1, -1):
                if h:

                    @pl.when(held(way, h))
                    def _():
                        hop(way, h - 1).wait_recv()

                if h < n_row - 1:

                    @pl.when(held(way, h) & onward(way))
                    def _():
                        hop(way, h).start()

        for h in range(n_row - 1):
            for way in (1, -1):

                @pl.when(held(way, h) & onward(way))
                def _():
                    hop(way, h).wait_send()

    def gather_chips(phase):
        core = lax.rem(me["col"], 2)
        chip = me["col"] // 2
        copies, passed = [], []

        def across(e):
            at = share("col", me["col"])
            copy = pltpu.make_async_remote_copy(
                src_ref=gath.at[phase, at], dst_ref=gath.at[phase, at],
                send_sem=ag_send.at[phase, 0, e], recv_sem=ag_recv.at[phase, 0, e],
                device_id={"col": 2 * lax.rem(chip + e, chips) + core},
                device_id_type=pl.DeviceIdType.MESH)
            copy.start()
            return copy

        def pass_on(e):
            at = share("col", 2 * lax.rem(chip + chips - e, chips) + core)
            copy = pltpu.make_async_remote_copy(
                src_ref=gath.at[phase, at], dst_ref=gath.at[phase, at],
                send_sem=ac_send.at[phase, e], recv_sem=ac_recv.at[phase, e],
                device_id={"col": 2 * chip + 1 - core},
                device_id_type=pl.DeviceIdType.MESH)
            copy.start()
            return copy

        for e in range(1, chips):
            copies.append(across(e))
        passed.append(pass_on(0))
        yield
        for e in range(1, chips):
            copies[e - 1].wait_recv()
            passed.append(pass_on(e))
        yield
        for copy in passed:
            copy.wait()
        for copy in copies:
            copy.wait_send()

    def gather(phase, axis, squares):
        sums = send_squares(
            axis, squares, stat_send.at[phase], stat_gather.at[phase], sa_send.at[phase], sa_recv.at[phase])
        yield from (gather_line if axis == "row" else gather_chips)(phase)
        return add_squares(axis, squares, stat_gather.at[phase], sums)

    def multiply(phase, direction):
        contract = (((1,), (0,)), ((), ())) if direction == 0 else (((1,), (1,)), ((), ()))

        def read(q):
            four = [4 * q + k for k in range(4)]
            xs = [gath[phase, idx[4 * direction + 1, p]] for p in four]
            corners = [blocks[idx[4 * direction, p]] for p in four]
            blank = jnp.zeros_like(xs[0])
            left = jnp.concatenate(
                [jnp.concatenate([x, blank] if k % 2 == 0 else [blank, x], axis=1) for k, x in enumerate(xs)],
                axis=0)
            if direction == 0:
                right = [jnp.concatenate([corners[k], corners[k + 2]], axis=1) for k in range(2)]
            else:
                right = [jnp.concatenate(corners[k : k + 2], axis=1) for k in (0, 2)]
            y = lax.dot_general(
                left, jnp.concatenate(right, axis=0), contract, preferred_element_type=jnp.float32)
            height = xs[0].shape[0]
            parts = [
                y[k * height : (k + 1) * height, (k // 2) * BS : (k // 2 + 1) * BS] for k in range(4)
            ]
            seconds = [keep[2 + direction, p] for p in four]
            return [
                part[:count_rhs] * (1.0 - second) + part[count_rhs:] * second
                for part, second in zip(parts, seconds)
            ]

        def write(q, ys, acc):
            for k, y in enumerate(ys):
                acc = acc * keep[direction, 4 * q + k] + y
                prods[4 * q + k] = acc
            return acc

        loop(slots // 4, read, write, jnp.zeros((count_rhs, BS), jnp.float32), 4)

    def partial(direction, at):
        first = idx[4 * direction + 2, 2 * at]
        second = idx[4 * direction + 2, 2 * at + 1]
        return jnp.concatenate([prods[first], prods[second]], axis=0)

    def fill_send(phase, direction, first, count, arrived=None):
        def read(j):
            value = partial(direction, first + j)
            if arrived is not None:
                value = value + arrived(j)
            return value.astype(jnp.bfloat16)

        def write(j, value, carry):
            send[phase, first + j] = value

        loop(count, read, write)

    def scatter_line(phase):
        w = width["row"]
        me_row = me["row"]
        odd = lax.rem(me_row, 2)
        pair = me_row // 2
        partner = me_row + 1 - 2 * odd
        recv = recv_row.at[phase // 2]

        def leg(at, device, target, send_sem, recv_sem):
            return pltpu.make_async_remote_copy(
                src_ref=send.at[phase, share("row", at)], dst_ref=target,
                send_sem=send_sem, recv_sem=recv_sem,
                device_id={"row": device}, device_id_type=pl.DeviceIdType.MESH)

        def outer(i, upward):
            at = lax.select(upward, n_row - 1 - i, i)
            return at, lax.select(upward, at > 2 * pair + 1, at < 2 * pair)

        def first_leg(i):
            at, there = outer(i, odd == 0)
            return at, there, leg(
                at, partner, transit.at[phase // 2, i], tr_send.at[phase // 2, i], tr_recv.at[phase // 2, i])

        def second_leg(i):
            at, there = outer(i, odd == 1)
            return at, there, leg(
                at, at, recv.at[pair], rs_send.at[phase, 1 + i], rs_recv.at[phase, pair])

        for i in range(n_row - 2):
            at, there, copy = first_leg(i)

            @pl.when(there)
            def _():
                fill_send(phase, 0, at * w, w)
                copy.start()

        fill_send(phase, 0, partner * w, w)
        direct = leg(partner, partner, recv.at[pair], rs_send.at[phase, 0], rs_recv.at[phase, pair])
        direct.start()

        def keep_own(j, value, carry):
            own[j] = value

        loop(w, lambda j: partial(0, me_row * w + j), keep_own)
        for i in range(n_row - 2):
            yield
            at, there, copy = second_leg(i)

            @pl.when(there)
            def _():
                pltpu.make_async_remote_copy(
                    src_ref=transit.at[phase // 2, i], dst_ref=transit.at[phase // 2, i],
                    send_sem=tr_send.at[phase // 2, i], recv_sem=tr_recv.at[phase // 2, i],
                    device_id={"row": partner}, device_id_type=pl.DeviceIdType.MESH).wait_recv()
                fill_send(phase, 0, at * w, w, lambda j: transit[phase // 2, i, j].astype(jnp.float32))
                copy.start()

        yield
        for m in range(n_row // 2):
            leg(partner, partner, recv.at[m], rs_send.at[phase, 0], rs_recv.at[phase, m]).wait_recv()
        direct.wait_send()
        for i in range(n_row - 2):
            for at, there, copy in (first_leg(i), second_leg(i)):

                @pl.when(there)
                def _():
                    copy.wait_send()

    def scatter_chips(phase):
        w = width["col"]
        core = lax.rem(me["col"], 2)
        chip = me["col"] // 2
        between, across = [], []
        for e in [*range(1, chips), 0]:
            first = (2 * lax.rem(chip + e, chips) + 1 - core) * w

            def stage(j, value, carry):
                core_send[phase // 2, e, j] = value

            loop(w, lambda j: partial(1, first + j), stage)
            copy = pltpu.make_async_remote_copy(
                src_ref=core_send.at[phase // 2, e], dst_ref=core_recv.at[phase // 2, e],
                send_sem=tr_send.at[ITERS + 1 + phase // 2, e], recv_sem=tr_recv.at[ITERS + 1 + phase // 2, e],
                device_id={"col": 2 * chip + 1 - core}, device_id_type=pl.DeviceIdType.MESH)
            copy.start()
            between.append(copy)
        yield
        for e in range(1, chips):
            to = 2 * lax.rem(chip + e, chips) + core
            between[e - 1].wait_recv()
            fill_send(phase, 1, to * w, w, lambda j: core_recv[phase // 2, e, j])
            copy = pltpu.make_async_remote_copy(
                src_ref=send.at[phase, share("col", to)], dst_ref=recv_col.at[phase // 2, e],
                send_sem=rs_send.at[phase, e], recv_sem=rs_recv.at[phase, e],
                device_id={"col": to}, device_id_type=pl.DeviceIdType.MESH)
            copy.start()
            across.append(copy)
        between[-1].wait_recv()

        def keep_own(j, value, carry):
            own[j] = value

        loop(w, lambda j: partial(1, me["col"] * w + j) + core_recv[phase // 2, 0, j], keep_own)
        yield
        for copy in across:
            copy.wait()
        for copy in between:
            copy.wait_send()

    def scatter(phase, axis, squares):
        target = stat_row if axis == "row" else stat_col
        sums = send_squares(
            axis, squares, stat_reduce.at[phase], target.at[phase // 2], sr_send.at[phase], sr_recv.at[phase])
        yield from (scatter_line if axis == "row" else scatter_chips)(phase)
        return add_squares(axis, squares, target.at[phase // 2], sums)

    def norm(squares):
        total = jnp.sum(squares[:count_rhs] + squares[count_rhs:], axis=1, keepdims=True) + norm_eps
        value = jnp.broadcast_to(jnp.sqrt(total), (count_rhs, BS))
        return jnp.concatenate([value, value], axis=0)

    def everywhere(which, squares):
        for at, axis in enumerate(("row", "col")):
            slot, sem = phases + 2 * which + at, 2 * which + at
            sums = send_squares(
                axis, squares, stat_send.at[slot], stat_gather.at[slot], fin_send.at[sem], fin_recv.at[sem])
            yield
            squares = add_squares(axis, squares, stat_gather.at[slot], sums)
        return squares

    def update(phase, axis, recv, scale, store, previous, gather_phase):
        first = me[axis] * width[axis]

        def read(j):
            total = own[j]
            for d in range(n_row // 2) if axis == "row" else range(1, chips):
                total = total + recv[phase // 2, d, j].astype(jnp.float32)
            return total * scale - previous(j)

        def write(j, value, squares):
            store[j] = value
            if gather_phase is not None:
                gath[gather_phase, first + j] = value.astype(jnp.bfloat16)
            return squares + value * value

        return loop(width[axis], read, write, jnp.zeros(tile, jnp.float32))

    zeros = jnp.zeros(tile, jnp.float32)
    prods[slots] = zeros[:count_rhs]
    ray_now, ray_next = ray_a, ray_b
    first_ray = me["col"] * width["col"]

    def travel_times(j):
        lanes = [slice((2 * j + k) * BS, (2 * j + k + 1) * BS) for k in range(2)]
        return jnp.concatenate([t_ref[mine, lanes[0]], t_ref[mine, lanes[1]]], axis=0)

    squares = zeros
    for j in range(width["col"]):
        value = travel_times(j)
        squares = squares + value * value
    squares = yield from everywhere(0, squares)
    beta = norm(squares)
    for j in range(width["col"]):
        value = travel_times(j)
        ray_now[j] = value
        gath[0, first_ray + j] = (value / beta).astype(jnp.bfloat16)

    squares = yield from gather(0, "col", zeros)
    if load is not None:
        load.wait()
    multiply(0, 0)
    yield from scatter(0, "row", squares)
    phi_bar = beta
    betas, alphas = [beta], []
    squares = update(0, "row", recv_row, 1.0, cells.at[0], lambda j: 0.0, 1)
    for iteration in range(ITERS):
        phase = 2 * iteration + 1
        squares = yield from gather(phase, "row", squares)
        multiply(phase, 1)
        alpha = norm((yield from scatter(phase, "col", squares)))
        alphas.append(alpha)
        turn = alpha / beta
        squares = update(
            phase, "col", recv_col, 1.0 / alpha, ray_next, lambda j: ray_now[j] * turn, phase + 1)
        ray_now, ray_next = ray_next, ray_now
        phase = phase + 1
        squares = yield from gather(phase, "col", squares)
        multiply(phase, 0)
        beta = norm((yield from scatter(phase, "row", squares)))
        betas.append(beta)
        turn = beta / alpha
        final = iteration == ITERS - 1
        squares = update(
            phase, "row", recv_row, 1.0 / beta, cells.at[iteration + 1],
            lambda j: cells[iteration, j] * turn, None if final else phase + 1)

    squares = yield from everywhere(1, squares)
    alphas.append(norm(squares))

    rho_bar = alphas[0]
    rates, turns = [], []
    for iteration in range(ITERS):
        rate, turn, rho_bar, phi_bar = rotation(
            rho_bar, phi_bar, betas[iteration + 1], alphas[iteration + 1])
        rates.append(rate)
        turns.append(turn)

    def finish(j):
        direction = cells[0, j] / alphas[0]
        total = zeros
        for iteration in range(ITERS):
            total = total + rates[iteration] * direction
            direction = cells[iteration + 1, j] / alphas[iteration + 1] - turns[iteration] * direction
        return total, phi_bar * direction

    def emit(j, values, carry):
        for k in range(2):
            lanes = pl.ds(pl.multiple_of((2 * j + k) * BS, BS), BS)
            rows = slice(k * count_rhs, (k + 1) * count_rhs)
            sol_ref[mine, lanes], dir_ref[mine, lanes] = values[0][rows], values[1][rows]

    loop(width["row"], finish, emit, step=4)


def order(key, other, filled):
    slots = key.shape[0]
    at = jnp.arange(slots, dtype=jnp.int32)
    key = jnp.where(filled, key, RB_DEV)
    other = jnp.where(filled, other, 0)
    before = (key[None, :] < key[:, None]) | ((key[None, :] == key[:, None]) & (at[None, :] < at[:, None]))
    rank = jnp.sum(before.astype(jnp.int32), axis=1)
    hot = (rank[None, :] == at[:, None]).astype(jnp.int32)
    perm = jnp.sum(hot * at[None, :], axis=1)
    other_sorted = jnp.sum(hot * other[None, :], axis=1)
    key_sorted = jnp.sum(hot * key[None, :], axis=1)
    same = jnp.concatenate([jnp.zeros((1,), bool), key_sorted[1:] == key_sorted[:-1]])
    outs = jnp.arange(RB_DEV, dtype=jnp.int32)[:, None]
    upto = jnp.sum((key[None, :] <= outs).astype(jnp.int32), axis=1)
    here = jnp.any(key[None, :] == outs, axis=1)
    last = jnp.where(here, upto - 1, slots)
    pad = RB_DEV - slots
    return (
        [jnp.pad(perm, (0, pad)), jnp.pad(other_sorted // 2, (0, pad)), last, last],
        jnp.pad(same.astype(jnp.float32), (0, pad)),
        jnp.pad((other_sorted % 2).astype(jnp.float32), (0, pad)),
    )


def shards(n_row, n_col, blocks, block_rows, block_cols, counts, travel_times):
    blocks_here = blocks[0, 0]
    rows_here = block_rows[0, 0]
    cols_here = block_cols[0, 0]
    slots = blocks_here.shape[0]
    count_rhs = travel_times.shape[0]
    filled = jnp.arange(slots, dtype=jnp.int32) < counts[0, 0]
    back, back_keep, back_second = order(cols_here, rows_here, filled)
    forth, forth_keep, forth_second = order(rows_here, cols_here, filled)
    idx = jnp.stack(back + forth)
    keep = jnp.stack([back_keep, forth_keep, back_second, forth_second])

    phases = 2 * ITERS + 1
    w_row, w_col = CB_DEV // n_row // 2, RB_DEV // n_col // 2
    n_max = max(n_row, n_col)
    tile = (2 * count_rhs // HALVES, BS)
    vmem, dma = pltpu.VMEM, pltpu.SemaphoreType.DMA
    f32, bf16 = jnp.float32, jnp.bfloat16
    out = jax.ShapeDtypeStruct((count_rhs, 2 * w_row * BS), f32)
    sol, direction = pl.pallas_call(
        functools.partial(kernel, n_row, n_col),
        out_shape=(out, out),
        in_specs=[
            pl.BlockSpec(memory_space=pltpu.SMEM),
            pl.BlockSpec(memory_space=pltpu.SMEM),
            pl.BlockSpec(memory_space=pl.ANY),
            pl.BlockSpec(memory_space=pltpu.VMEM),
        ],
        out_specs=(pl.BlockSpec(memory_space=pltpu.VMEM),) * 2,
        scratch_shapes=[
            vmem(blocks_here.shape, bf16),
            dma,
            *[vmem((phases, RB_DEV // 2, *tile), bf16)] * HALVES,
            vmem((HALVES, slots + 1, count_rhs // HALVES, BS), f32),
            vmem((HALVES, max(w_row, w_col), *tile), f32),
            vmem((HALVES, w_col, *tile), f32),
            vmem((HALVES, w_col, *tile), f32),
            vmem((HALVES, ITERS + 1, w_row, *tile), f32),
            vmem((HALVES, phases, RB_DEV // 2, *tile), bf16),
            vmem((HALVES, ITERS + 1, n_row - 2, w_row, *tile), bf16),
            vmem((HALVES, ITERS + 1, n_row // 2, w_row, *tile), bf16),
            vmem((HALVES, ITERS, n_col // 2, w_col, *tile), f32),
            vmem((HALVES, ITERS, n_col // 2, w_col, *tile), f32),
            vmem((HALVES, ITERS, n_col // 2, w_col, *tile), bf16),
            vmem((HALVES, phases + 4, *tile), f32),
            vmem((HALVES, phases + 4, n_max, *tile), f32),
            vmem((HALVES, phases, *tile), f32),
            vmem((HALVES, ITERS + 1, n_row, *tile), f32),
            vmem((HALVES, ITERS, n_col, *tile), f32),
            *[dma((HALVES, phases, 2, n_max))] * 2,
            *[dma((HALVES, phases, n_max))] * 4,
            *[dma((HALVES, 2 * ITERS + 1, n_max))] * 2,
            *[dma((HALVES, phases, n_max))] * 4,
            *[dma((HALVES, 4, n_max))] * 2,
        ],
        compiler_params=pltpu.CompilerParams(
            collective_id=0, has_side_effects=True, vmem_limit_bytes=48 * 1024 * 1024
        ),
    )(idx, keep, blocks_here, travel_times)
    return (sol.reshape(count_rhs, 1, 1, -1), direction.reshape(count_rhs, 1, 1, -1))


def solution(mesh):
    placed = (
        P("row", "col", None, None, None),
        P("row", "col", None),
        P("row", "col", None),
        P("row", "col"),
        P(None, ("row", "col")),
    )
    return jax.shard_map(
        functools.partial(shards, mesh.shape["row"], mesh.shape["col"]),
        mesh=mesh,
        in_specs=placed,
        out_specs=(P(None, "col", "row", None), P(None, "col", "row", None)),
        check_vma=False,
    )
```

```python
import functools

import jax
import jax.numpy as jnp
from jax import lax
from jax.experimental import pallas as pl
from jax.experimental.pallas import tpu as pltpu
from jax.sharding import PartitionSpec as P

BS = 128
RB_DEV = 256
CB_DEV = 256
ITERS = 2
UNROLL = 8
HALVES = 2
TOGETHER = 5
LEAD = 3

norm_eps = 1e-06


def rotation(rho_bar, phi_bar, beta_norm, alpha_norm):
    rho_new = jnp.sqrt(rho_bar * rho_bar + beta_norm * beta_norm)
    cosine = rho_bar / rho_new
    sine_val = beta_norm / rho_new
    theta_coef = sine_val * alpha_norm
    rho_next = -cosine * alpha_norm
    phi_new = cosine * phi_bar
    phi_next = sine_val * phi_bar
    return (phi_new / rho_new, theta_coef / rho_new, rho_next, phi_next)


def loop(count, read, write, init=None, step=UNROLL):
    while count % step:
        step //= 2

    def several(chunk, carry):
        values = [read(chunk * step + k) for k in range(step)]
        for k in range(step):
            carry = write(chunk * step + k, values[k], carry)
        return carry

    return lax.fori_loop(0, count // step, several, init)


def kernel(
    n_row, n_col, idx, keep, blocks_hbm, t_ref, sol_ref, dir_ref, blocks, load_sem, *scratch
):
    gaths, scratch = scratch[:HALVES], scratch[HALVES:]
    size = {"row": n_row, "col": n_col}
    load = pltpu.make_async_copy(blocks_hbm, blocks, load_sem)
    load.start()

    barrier = pltpu.get_barrier_semaphore()
    for axis in size:
        for d in range(1, size[axis]):
            pl.semaphore_signal(
                barrier, inc=1, device_id={axis: lax.rem(lax.axis_index(axis) + d, size[axis])},
                device_id_type=pl.DeviceIdType.MESH,
            )
    pl.semaphore_wait(barrier, n_row + n_col - 2)

    programs = [
        half(g, n_row, n_col, load if g == 0 else None, idx, keep, t_ref, sol_ref, dir_ref, blocks,
             gaths[g], *[ref.at[g] for ref in scratch])
        for g in range(HALVES)
    ]
    for _ in range(TOGETHER):
        for program in programs:
            next(program)
    for _ in range(LEAD):
        next(programs[0])
    while programs:
        programs = [program for program in programs if next(program, True) is None]


def half(
    g, n_row, n_col, load, idx, keep, t_ref, sol_ref, dir_ref, blocks,
    gath, prods, own, ray_a, ray_b, cells, send, transit, recv_row, core_send, core_recv, recv_col,
    stat_send, stat_gather, stat_reduce, stat_row, stat_col,
    ag_send, ag_recv, ac_send, ac_recv, sa_send, sa_recv,
    tr_send, tr_recv, rs_send, rs_recv, sr_send, sr_recv, fin_send, fin_recv,
):
    phases = 2 * ITERS + 1
    slots = blocks.shape[0]
    count_rhs = t_ref.shape[0] // HALVES
    tile = (2 * count_rhs, BS)
    mine = slice(g * count_rhs, (g + 1) * count_rhs)
    size = {"row": n_row, "col": n_col}
    me = {axis: lax.axis_index(axis) for axis in size}
    width = {"row": CB_DEV // n_row // 2, "col": RB_DEV // n_col // 2}

    chips = n_col // 2

    def peer(axis, d):
        return {axis: lax.rem(me[axis] + d, size[axis])}

    def push(src, dst, send_sem, recv_sem, axis, d):
        copy = pltpu.make_async_remote_copy(
            src_ref=src, dst_ref=dst, send_sem=send_sem, recv_sem=recv_sem,
            device_id=peer(axis, d), device_id_type=pl.DeviceIdType.MESH,
        )
        copy.start()
        return copy

    def share(axis, at):
        return pl.ds(pl.multiple_of(at * width[axis], width[axis]), width[axis])

    def send_squares(axis, squares, source, target, send_sem, recv_sem):
        source[...] = squares
        return [
            push(source, target.at[d], send_sem.at[d], recv_sem.at[d], axis, d)
            for d in range(1, size[axis])
        ]

    def add_squares(axis, squares, target, copies):
        for copy in copies:
            copy.wait()
        for d in range(1, size[axis]):
            squares = squares + target[d]
        return squares

    def gather_line(phase):
        me_row = me["row"]

        def hop(way, h):
            at = share("row", jnp.clip(me_row - way * h, 0, n_row - 1))
            lane = 0 if way > 0 else 1
            return pltpu.make_async_remote_copy(
                src_ref=gath.at[phase, at], dst_ref=gath.at[phase, at],
                send_sem=ag_send.at[phase, lane, h], recv_sem=ag_recv.at[phase, lane, h],
                device_id={"row": jnp.clip(me_row + way, 0, n_row - 1)},
                device_id_type=pl.DeviceIdType.MESH)

        def held(way, h):
            return (me_row >= h) if way > 0 else (me_row + h < n_row)

        def onward(way):
            return (me_row < n_row - 1) if way > 0 else (me_row > 0)

        for h in range(n_row):
            if h:
                yield
            for way in (1, -1):
                if h:

                    @pl.when(held(way, h))
                    def _():
                        hop(way, h - 1).wait_recv()

                if h < n_row - 1:

                    @pl.when(held(way, h) & onward(way))
                    def _():
                        hop(way, h).start()

        for h in range(n_row - 1):
            for way in (1, -1):

                @pl.when(held(way, h) & onward(way))
                def _():
                    hop(way, h).wait_send()

    def gather_chips(phase):
        core = lax.rem(me["col"], 2)
        chip = me["col"] // 2
        copies, passed = [], []

        def across(e):
            at = share("col", me["col"])
            copy = pltpu.make_async_remote_copy(
                src_ref=gath.at[phase, at], dst_ref=gath.at[phase, at],
                send_sem=ag_send.at[phase, 0, e], recv_sem=ag_recv.at[phase, 0, e],
                device_id={"col": 2 * lax.rem(chip + e, chips) + core},
                device_id_type=pl.DeviceIdType.MESH)
            copy.start()
            return copy

        def pass_on(e):
            at = share("col", 2 * lax.rem(chip + chips - e, chips) + core)
            copy = pltpu.make_async_remote_copy(
                src_ref=gath.at[phase, at], dst_ref=gath.at[phase, at],
                send_sem=ac_send.at[phase, e], recv_sem=ac_recv.at[phase, e],
                device_id={"col": 2 * chip + 1 - core},
                device_id_type=pl.DeviceIdType.MESH)
            copy.start()
            return copy

        for e in range(1, chips):
            copies.append(across(e))
        passed.append(pass_on(0))
        yield
        for e in range(1, chips):
            copies[e - 1].wait_recv()
            passed.append(pass_on(e))
        yield
        for copy in passed:
            copy.wait()
        for copy in copies:
            copy.wait_send()

    def gather(phase, axis, squares):
        sums = send_squares(
            axis, squares, stat_send.at[phase], stat_gather.at[phase], sa_send.at[phase], sa_recv.at[phase])
        yield from (gather_line if axis == "row" else gather_chips)(phase)
        return add_squares(axis, squares, stat_gather.at[phase], sums)

    def multiply(phase, direction):
        contract = (((1,), (0,)), ((), ())) if direction == 0 else (((1,), (1,)), ((), ()))

        def read(q):
            four = [4 * q + k for k in range(4)]
            xs = [gath[phase, idx[4 * direction + 1, p]] for p in four]
            corners = [blocks[idx[4 * direction, p]] for p in four]
            blank = jnp.zeros_like(xs[0])
            left = jnp.concatenate(
                [jnp.concatenate([x, blank] if k % 2 == 0 else [blank, x], axis=1) for k, x in enumerate(xs)],
                axis=0)
            if direction == 0:
                right = [jnp.concatenate([corners[k], corners[k + 2]], axis=1) for k in range(2)]
            else:
                right = [jnp.concatenate(corners[k : k + 2], axis=1) for k in (0, 2)]
            y = lax.dot_general(
                left, jnp.concatenate(right, axis=0), contract, preferred_element_type=jnp.float32)
            height = xs[0].shape[0]
            parts = [
                y[k * height : (k + 1) * height, (k // 2) * BS : (k // 2 + 1) * BS] for k in range(4)
            ]
            seconds = [keep[2 + direction, p] for p in four]
            return [
                part[:count_rhs] * (1.0 - second) + part[count_rhs:] * second
                for part, second in zip(parts, seconds)
            ]

        def write(q, ys, acc):
            for k, y in enumerate(ys):
                acc = acc * keep[direction, 4 * q + k] + y
                prods[4 * q + k] = acc
            return acc

        acc = jnp.zeros((count_rhs, BS), jnp.float32)
        fours = slots // 4
        middle = fours // 8 * 4
        acc = loop(middle, read, write, acc, 4)
        yield
        loop(fours - middle, lambda q: read(middle + q), lambda q, ys, acc: write(middle + q, ys, acc), acc, 4)

    def partial(direction, at):
        first = idx[4 * direction + 2, 2 * at]
        second = idx[4 * direction + 2, 2 * at + 1]
        return jnp.concatenate([prods[first], prods[second]], axis=0)

    def fill_send(phase, direction, first, count, arrived=None):
        def read(j):
            value = partial(direction, first + j)
            if arrived is not None:
                value = value + arrived(j)
            return value.astype(jnp.bfloat16)

        def write(j, value, carry):
            send[phase, first + j] = value

        loop(count, read, write)

    def scatter_line(phase):
        w = width["row"]
        me_row = me["row"]
        odd = lax.rem(me_row, 2)
        pair = me_row // 2
        partner = me_row + 1 - 2 * odd
        recv = recv_row.at[phase // 2]

        def leg(at, device, target, send_sem, recv_sem):
            return pltpu.make_async_remote_copy(
                src_ref=send.at[phase, share("row", at)], dst_ref=target,
                send_sem=send_sem, recv_sem=recv_sem,
                device_id={"row": device}, device_id_type=pl.DeviceIdType.MESH)

        def outer(i, upward):
            at = lax.select(upward, n_row - 1 - i, i)
            return at, lax.select(upward, at > 2 * pair + 1, at < 2 * pair)

        def first_leg(i):
            at, there = outer(i, odd == 0)
            return at, there, leg(
                at, partner, transit.at[phase // 2, i], tr_send.at[phase // 2, i], tr_recv.at[phase // 2, i])

        def second_leg(i):
            at, there = outer(i, odd == 1)
            return at, there, leg(
                at, at, recv.at[pair], rs_send.at[phase, 1 + i], rs_recv.at[phase, pair])

        for i in range(n_row - 2):
            at, there, copy = first_leg(i)

            @pl.when(there)
            def _():
                fill_send(phase, 0, at * w, w)
                copy.start()

        fill_send(phase, 0, partner * w, w)
        direct = leg(partner, partner, recv.at[pair], rs_send.at[phase, 0], rs_recv.at[phase, pair])
        direct.start()

        def keep_own(j, value, carry):
            own[j] = value

        loop(w, lambda j: partial(0, me_row * w + j), keep_own)
        for i in range(n_row - 2):
            yield
            at, there, copy = second_leg(i)

            @pl.when(there)
            def _():
                pltpu.make_async_remote_copy(
                    src_ref=transit.at[phase // 2, i], dst_ref=transit.at[phase // 2, i],
                    send_sem=tr_send.at[phase // 2, i], recv_sem=tr_recv.at[phase // 2, i],
                    device_id={"row": partner}, device_id_type=pl.DeviceIdType.MESH).wait_recv()
                fill_send(phase, 0, at * w, w, lambda j: transit[phase // 2, i, j].astype(jnp.float32))
                copy.start()

        yield
        for m in range(n_row // 2):
            leg(partner, partner, recv.at[m], rs_send.at[phase, 0], rs_recv.at[phase, m]).wait_recv()
        direct.wait_send()
        for i in range(n_row - 2):
            for at, there, copy in (first_leg(i), second_leg(i)):

                @pl.when(there)
                def _():
                    copy.wait_send()

    def scatter_chips(phase):
        w = width["col"]
        core = lax.rem(me["col"], 2)
        chip = me["col"] // 2
        between, across = [], []
        for e in [*range(1, chips), 0]:
            first = (2 * lax.rem(chip + e, chips) + 1 - core) * w

            def stage(j, value, carry):
                core_send[phase // 2, e, j] = value

            loop(w, lambda j: partial(1, first + j), stage)
            copy = pltpu.make_async_remote_copy(
                src_ref=core_send.at[phase // 2, e], dst_ref=core_recv.at[phase // 2, e],
                send_sem=tr_send.at[ITERS + 1 + phase // 2, e], recv_sem=tr_recv.at[ITERS + 1 + phase // 2, e],
                device_id={"col": 2 * chip + 1 - core}, device_id_type=pl.DeviceIdType.MESH)
            copy.start()
            between.append(copy)
        yield
        for e in range(1, chips):
            to = 2 * lax.rem(chip + e, chips) + core
            between[e - 1].wait_recv()
            fill_send(phase, 1, to * w, w, lambda j: core_recv[phase // 2, e, j])
            copy = pltpu.make_async_remote_copy(
                src_ref=send.at[phase, share("col", to)], dst_ref=recv_col.at[phase // 2, e],
                send_sem=rs_send.at[phase, e], recv_sem=rs_recv.at[phase, e],
                device_id={"col": to}, device_id_type=pl.DeviceIdType.MESH)
            copy.start()
            across.append(copy)
        between[-1].wait_recv()

        def keep_own(j, value, carry):
            own[j] = value

        loop(w, lambda j: partial(1, me["col"] * w + j) + core_recv[phase // 2, 0, j], keep_own)
        yield
        for copy in across:
            copy.wait()
        for copy in between:
            copy.wait_send()

    def scatter(phase, axis, squares):
        target = stat_row if axis == "row" else stat_col
        sums = send_squares(
            axis, squares, stat_reduce.at[phase], target.at[phase // 2], sr_send.at[phase], sr_recv.at[phase])
        yield from (scatter_line if axis == "row" else scatter_chips)(phase)
        return add_squares(axis, squares, target.at[phase // 2], sums)

    def norm(squares):
        total = jnp.sum(squares[:count_rhs] + squares[count_rhs:], axis=1, keepdims=True) + norm_eps
        value = jnp.broadcast_to(jnp.sqrt(total), (count_rhs, BS))
        return jnp.concatenate([value, value], axis=0)

    def everywhere(which, squares):
        for at, axis in enumerate(("row", "col")):
            slot, sem = phases + 2 * which + at, 2 * which + at
            sums = send_squares(
                axis, squares, stat_send.at[slot], stat_gather.at[slot], fin_send.at[sem], fin_recv.at[sem])
            yield
            squares = add_squares(axis, squares, stat_gather.at[slot], sums)
        return squares

    def update(phase, axis, recv, scale, store, previous, gather_phase):
        first = me[axis] * width[axis]

        def read(j):
            total = own[j]
            for d in range(n_row // 2) if axis == "row" else range(1, chips):
                total = total + recv[phase // 2, d, j].astype(jnp.float32)
            return total * scale - previous(j)

        def write(j, value, squares):
            store[j] = value
            if gather_phase is not None:
                gath[gather_phase, first + j] = value.astype(jnp.bfloat16)
            return squares + value * value

        return loop(width[axis], read, write, jnp.zeros(tile, jnp.float32))

    zeros = jnp.zeros(tile, jnp.float32)
    prods[slots] = zeros[:count_rhs]
    ray_now, ray_next = ray_a, ray_b
    first_ray = me["col"] * width["col"]

    def travel_times(j):
        lanes = [slice((2 * j + k) * BS, (2 * j + k + 1) * BS) for k in range(2)]
        return jnp.concatenate([t_ref[mine, lanes[0]], t_ref[mine, lanes[1]]], axis=0)

    squares = zeros
    for j in range(width["col"]):
        value = travel_times(j)
        squares = squares + value * value
    squares = yield from everywhere(0, squares)
    beta = norm(squares)
    for j in range(width["col"]):
        value = travel_times(j)
        ray_now[j] = value
        gath[0, first_ray + j] = (value / beta).astype(jnp.bfloat16)

    squares = yield from gather(0, "col", zeros)
    if load is not None:
        load.wait()
    yield from multiply(0, 0)
    yield from scatter(0, "row", squares)
    phi_bar = beta
    betas, alphas = [beta], []
    squares = update(0, "row", recv_row, 1.0, cells.at[0], lambda j: 0.0, 1)
    for iteration in range(ITERS):
        phase = 2 * iteration + 1
        squares = yield from gather(phase, "row", squares)
        yield from multiply(phase, 1)
        alpha = norm((yield from scatter(phase, "col", squares)))
        alphas.append(alpha)
        turn = alpha / beta
        squares = update(
            phase, "col", recv_col, 1.0 / alpha, ray_next, lambda j: ray_now[j] * turn, phase + 1)
        ray_now, ray_next = ray_next, ray_now
        phase = phase + 1
        squares = yield from gather(phase, "col", squares)
        yield from multiply(phase, 0)
        beta = norm((yield from scatter(phase, "row", squares)))
        betas.append(beta)
        turn = beta / alpha
        final = iteration == ITERS - 1
        squares = update(
            phase, "row", recv_row, 1.0 / beta, cells.at[iteration + 1],
            lambda j: cells[iteration, j] * turn, None if final else phase + 1)

    squares = yield from everywhere(1, squares)
    alphas.append(norm(squares))

    rho_bar = alphas[0]
    rates, turns = [], []
    for iteration in range(ITERS):
        rate, turn, rho_bar, phi_bar = rotation(
            rho_bar, phi_bar, betas[iteration + 1], alphas[iteration + 1])
        rates.append(rate)
        turns.append(turn)

    def finish(j):
        direction = cells[0, j] / alphas[0]
        total = zeros
        for iteration in range(ITERS):
            total = total + rates[iteration] * direction
            direction = cells[iteration + 1, j] / alphas[iteration + 1] - turns[iteration] * direction
        return total, phi_bar * direction

    def emit(j, values, carry):
        for k in range(2):
            lanes = pl.ds(pl.multiple_of((2 * j + k) * BS, BS), BS)
            rows = slice(k * count_rhs, (k + 1) * count_rhs)
            sol_ref[mine, lanes], dir_ref[mine, lanes] = values[0][rows], values[1][rows]

    loop(width["row"], finish, emit, step=4)


def order(key, other, filled):
    slots = key.shape[0]
    at = jnp.arange(slots, dtype=jnp.int32)
    key = jnp.where(filled, key, RB_DEV)
    other = jnp.where(filled, other, 0)
    before = (key[None, :] < key[:, None]) | ((key[None, :] == key[:, None]) & (at[None, :] < at[:, None]))
    rank = jnp.sum(before.astype(jnp.int32), axis=1)
    hot = (rank[None, :] == at[:, None]).astype(jnp.int32)
    perm = jnp.sum(hot * at[None, :], axis=1)
    other_sorted = jnp.sum(hot * other[None, :], axis=1)
    key_sorted = jnp.sum(hot * key[None, :], axis=1)
    same = jnp.concatenate([jnp.zeros((1,), bool), key_sorted[1:] == key_sorted[:-1]])
    outs = jnp.arange(RB_DEV, dtype=jnp.int32)[:, None]
    upto = jnp.sum((key[None, :] <= outs).astype(jnp.int32), axis=1)
    here = jnp.any(key[None, :] == outs, axis=1)
    last = jnp.where(here, upto - 1, slots)
    pad = RB_DEV - slots
    return (
        [jnp.pad(perm, (0, pad)), jnp.pad(other_sorted // 2, (0, pad)), last, last],
        jnp.pad(same.astype(jnp.float32), (0, pad)),
        jnp.pad((other_sorted % 2).astype(jnp.float32), (0, pad)),
    )


def shards(n_row, n_col, blocks, block_rows, block_cols, counts, travel_times):
    blocks_here = blocks[0, 0]
    rows_here = block_rows[0, 0]
    cols_here = block_cols[0, 0]
    slots = blocks_here.shape[0]
    count_rhs = travel_times.shape[0]
    filled = jnp.arange(slots, dtype=jnp.int32) < counts[0, 0]
    back, back_keep, back_second = order(cols_here, rows_here, filled)
    forth, forth_keep, forth_second = order(rows_here, cols_here, filled)
    idx = jnp.stack(back + forth)
    keep = jnp.stack([back_keep, forth_keep, back_second, forth_second])

    phases = 2 * ITERS + 1
    w_row, w_col = CB_DEV // n_row // 2, RB_DEV // n_col // 2
    n_max = max(n_row, n_col)
    tile = (2 * count_rhs // HALVES, BS)
    vmem, dma = pltpu.VMEM, pltpu.SemaphoreType.DMA
    f32, bf16 = jnp.float32, jnp.bfloat16
    out = jax.ShapeDtypeStruct((count_rhs, 2 * w_row * BS), f32)
    sol, direction = pl.pallas_call(
        functools.partial(kernel, n_row, n_col),
        out_shape=(out, out),
        in_specs=[
            pl.BlockSpec(memory_space=pltpu.SMEM),
            pl.BlockSpec(memory_space=pltpu.SMEM),
            pl.BlockSpec(memory_space=pl.ANY),
            pl.BlockSpec(memory_space=pltpu.VMEM),
        ],
        out_specs=(pl.BlockSpec(memory_space=pltpu.VMEM),) * 2,
        scratch_shapes=[
            vmem(blocks_here.shape, bf16),
            dma,
            *[vmem((phases, RB_DEV // 2, *tile), bf16)] * HALVES,
            vmem((HALVES, slots + 1, count_rhs // HALVES, BS), f32),
            vmem((HALVES, max(w_row, w_col), *tile), f32),
            vmem((HALVES, w_col, *tile), f32),
            vmem((HALVES, w_col, *tile), f32),
            vmem((HALVES, ITERS + 1, w_row, *tile), f32),
            vmem((HALVES, phases, RB_DEV // 2, *tile), bf16),
            vmem((HALVES, ITERS + 1, n_row - 2, w_row, *tile), bf16),
            vmem((HALVES, ITERS + 1, n_row // 2, w_row, *tile), bf16),
            vmem((HALVES, ITERS, n_col // 2, w_col, *tile), f32),
            vmem((HALVES, ITERS, n_col // 2, w_col, *tile), f32),
            vmem((HALVES, ITERS, n_col // 2, w_col, *tile), bf16),
            vmem((HALVES, phases + 4, *tile), f32),
            vmem((HALVES, phases + 4, n_max, *tile), f32),
            vmem((HALVES, phases, *tile), f32),
            vmem((HALVES, ITERS + 1, n_row, *tile), f32),
            vmem((HALVES, ITERS, n_col, *tile), f32),
            *[dma((HALVES, phases, 2, n_max))] * 2,
            *[dma((HALVES, phases, n_max))] * 4,
            *[dma((HALVES, 2 * ITERS + 1, n_max))] * 2,
            *[dma((HALVES, phases, n_max))] * 4,
            *[dma((HALVES, 4, n_max))] * 2,
        ],
        compiler_params=pltpu.CompilerParams(
            collective_id=0, has_side_effects=True, vmem_limit_bytes=48 * 1024 * 1024
        ),
    )(idx, keep, blocks_here, travel_times)
    return (sol.reshape(count_rhs, 1, 1, -1), direction.reshape(count_rhs, 1, 1, -1))


def solution(mesh):
    placed = (
        P("row", "col", None, None, None),
        P("row", "col", None),
        P("row", "col", None),
        P("row", "col"),
        P(None, ("row", "col")),
    )
    return jax.shard_map(
        functools.partial(shards, mesh.shape["row"], mesh.shape["col"]),
        mesh=mesh,
        in_specs=placed,
        out_specs=(P(None, "col", "row", None), P(None, "col", "row", None)),
        check_vma=False,
    )
```
